32 devices in a mesh: rows: 32 (over z, y, x, core).
Axes of the slice: x: 2, y: 2, z: 4, core: 2. Of those that a mesh axis runs over, the one named last changes fastest.
Arguments:
- right_sides: float32 [65536, 512], P('rows'), may hold values from -6 to 6
- leaf_inverse: float32 [65536, 512], P('rows'), may hold values from -3 to 3, as said below
- mid_proj: float32 [65536, 256], P('rows'), may hold values from -0.046875 to 0.046875
- mid_basis: float32 [65536, 256], P('rows'), may hold values from -0.375 to 0.375
- mid_cap: float32 [2, 512, 512], replicated, may hold values from -3 to 3, as said below
- top_proj: float32 [65536, 256], P('rows'), may hold values from -0.03125 to 0.03125
- top_basis: float32 [65536, 256], P('rows'), may hold values from -0.375 to 0.375
- top_cap: float32 [1, 512, 512], replicated, may hold values from -3 to 3, as said below
Outputs:
- solution: float32 [65536, 512], P('rows')
The draws below stay inside these ranges and needn't reach their ends.
Inputs may be any that keep to these rules, and one draw needn't show every extreme that they name: `leaf_inverse`: each row's entry at its own position within its block is the largest. `mid_cap`: each row's diagonal entry is its largest. `top_cap`: each row's diagonal entry is its largest.
All inputs are finite; a program needn't handle non-finite values.
Results may differ from the reference program's by a relative error of at most 0.00014.
Values sent between devices are 32-bit elements; how exact they have to be, the bound alone decides.
A program may use at most 128 MiB of HBM per device.

```python
import jax
import jax.numpy as jnp
from jax import lax

RANK = 256
LEAF = 512
RHS = 512
NN = 65536


def dominant(key, count, order, spread, noise):
    key_diag, key_noise = jax.random.split(key)
    diag = jnp.exp(jax.random.uniform(key_diag, (count, 1), jnp.float32, -spread, spread))
    rough = jax.random.uniform(key_noise, (count, order), jnp.float32, -1.0, 1.0) * noise * (3.0 / order) ** 0.5
    return (diag, rough)


def draw_leaf_inverse(key, part):
    key = jax.random.fold_in(key, 11)
    spread, noise = (0.5, 0.3)
    diag, rough = dominant(key, NN, LEAF, spread, noise)
    places = jnp.arange(NN) % LEAF
    onehot = (places[:, None] == jnp.arange(LEAF)[None, :]).astype(jnp.float32)
    return onehot * diag + rough


def cap_matrix(key, count, spread, noise):
    order = 2 * RANK
    diag, rough = dominant(key, count * order, order, spread, noise)
    rough = rough.reshape(count, order, order)
    diag = diag.reshape(count, order, 1)
    eye_mat = (jnp.arange(order)[:, None] == jnp.arange(order)[None, :]).astype(jnp.float32)
    return eye_mat[None] * diag + rough


def draw_mid_cap(key, part):
    key = jax.random.fold_in(key, 23)
    return cap_matrix(key, 2, 0.5, 0.35)


def draw_top_cap(key, part):
    key = jax.random.fold_in(key, 37)
    return cap_matrix(key, 1, 0.5, 0.35)


def block_scale(key, dims, cuts, smallest, largest):
    factor_of = 1.0
    for axis_at, parts in cuts:
        heights = jax.random.uniform(jax.random.fold_in(jax.random.fold_in(key, 6), axis_at), (parts,), jnp.float32, smallest / len(cuts), largest / len(cuts))
        factor_of = factor_of * jnp.repeat(jnp.exp(heights), dims[axis_at] // parts).reshape((-1,) + (1,) * (len(dims) - 1 - axis_at))
    return factor_of


def centred(rng, shape, deviation, bound, cuts=(), kind=jnp.bfloat16):
    drawn = jax.random.normal(rng, shape, jnp.float32) * deviation
    if len(cuts) > 0:
        drawn = block_scale(rng, shape, cuts, -0.22, 0.18) * drawn
    return jnp.clip(drawn, min=-bound, max=bound).astype(kind)


def setup_inputs(seed: int = 0) -> dict:
    keys = jax.random.split(jax.random.key(seed), 9)
    right_sides = centred(keys[0], (NN, RHS), 1.0, 6.0, ((0, 32),), jnp.float32)
    leaf_inverse = draw_leaf_inverse(jax.random.fold_in(keys[8], 71), 0)
    mid_proj = centred(keys[2], (NN, RANK), (NN // 4) ** -0.5, 0.046875, ((0, 32),), jnp.float32)
    mid_basis = centred(keys[3], (NN, RANK), RANK ** -0.5, 0.375, ((0, 32),), jnp.float32)
    mid_cap = draw_mid_cap(jax.random.fold_in(keys[8], 71), 0)
    top_proj = centred(keys[5], (NN, RANK), (NN // 2) ** -0.5, 0.03125, ((0, 32),), jnp.float32)
    top_basis = centred(keys[6], (NN, RANK), RANK ** -0.5, 0.375, ((0, 32),), jnp.float32)
    top_cap = draw_top_cap(jax.random.fold_in(keys[8], 71), 0)
    return dict(right_sides=right_sides, leaf_inverse=leaf_inverse, mid_proj=mid_proj, mid_basis=mid_basis, mid_cap=mid_cap, top_proj=top_proj, top_basis=top_basis, top_cap=top_cap)


PRECISE = lax.Precision.HIGHEST


def leaf_apply(leaf_inverse, right_sides):
    block_count = right_sides.shape[0] // LEAF
    blocks = leaf_inverse.reshape(block_count, LEAF, LEAF)
    pieces = right_sides.reshape(block_count, LEAF, right_sides.shape[1])
    return jnp.einsum('bij,bjr->bir', blocks, pieces, precision=PRECISE).reshape(right_sides.shape)


def correct(field, factor, basis, capacity, pairs):
    half_rows = field.shape[0] // (2 * pairs)
    columns = field.shape[1]
    projection = jnp.einsum('gnk,gnr->gkr', factor.reshape(2 * pairs, half_rows, RANK), field.reshape(2 * pairs, half_rows, columns), precision=PRECISE)
    projection = projection.reshape(pairs, 2, RANK, columns)
    stacked = jnp.concatenate([projection[:, 1], projection[:, 0]], axis=1)
    coef = jnp.einsum('gij,gjr->gir', capacity, stacked, precision=PRECISE).reshape(2 * pairs, RANK, columns)
    fixing = jnp.einsum('gnk,gkr->gnr', basis.reshape(2 * pairs, half_rows, RANK), coef, precision=PRECISE)
    return field - fixing.reshape(field.shape)


def reference(right_sides, leaf_inverse, mid_proj, mid_basis, mid_cap, top_proj, top_basis, top_cap):
    leaf_out = leaf_apply(leaf_inverse, right_sides)
    mid_field = correct(leaf_out, mid_proj, mid_basis, mid_cap, 2)
    return correct(mid_field, top_proj, top_basis, top_cap, 1)
```

```python
import functools

import jax
import jax.numpy as jnp
from jax import lax
from jax.experimental import pallas as pl
from jax.experimental.pallas import tpu as pltpu
from jax.sharding import PartitionSpec as P

MESH = pl.DeviceIdType.MESH
GROUPS = 2
NN = (((1,), (0,)), ((), ()))
NT = (((1,), (1,)), ((), ()))


def split(value):
    high = value.astype(jnp.bfloat16)
    return high, (value - high.astype(jnp.float32)).astype(jnp.bfloat16)


def dot3(left, right, dims):
    def one(a, b):
        return lax.dot_general(a, b, dims, preferred_element_type=jnp.float32)

    return one(left[0], right[0]) + (one(left[0], right[1]) + one(left[1], right[0]))


def flip(number, mask):
    bit = 1
    while bit <= mask:
        if mask & bit:
            number = number + (1 - 2 * (number // bit % 2)) * bit
        bit *= 2
    return number


def coef_kernel(
    n, leaf, rank,
    rs_hbm, inv_hbm, vm_hbm, ym_hbm, mid_cap, vt_hbm, top_cap,
    field_out, coef_out,
    rs, inv, vm, vt, ym, cap, tcap, field,
    inv_h, inv_l, v_h, v_l, cap_h, cap_l, tcap_h, tcap_l, d_h, d_l,
    part, part_in, chip_sum, chip_in, pair, top_p, coef,
    d_part, d_part_in, d_sum, d_in, d_full,
    load_sem, cap_sem, out_sem, send_sem, recv_sem,
):
    m = n // 4
    chips = m // 2
    me = lax.axis_index("rows")
    quarter, place = me // m, me % m
    core, chip = place % 2, place // 2
    half, side = quarter // 2, quarter % 2
    partner = me + 1 - 2 * core
    sibling = me + m * (1 - 2 * side)
    across = me + 2 * m * (1 - 2 * half)
    rows, rhs = rs.shape
    blocks = rows // leaf
    cols = rhs // GROUPS
    hr = cols // 2
    w = cols // m
    wd = rank // m
    hd = rank // 2

    def on_chip(d):
        return me + 2 * (flip(chip, d) - chip)

    def ds(start, size):
        return pl.ds(pl.multiple_of(start, 8), size)

    loads = ((ym_hbm, ym), (vt_hbm, vt), (inv_hbm, inv), (rs_hbm, rs), (vm_hbm, vm))

    def load(k, b):
        src, dst = loads[k]
        at = pl.ds(b * leaf, leaf)
        return pltpu.make_async_copy(src.at[at], dst.at[at], load_sem.at[k, b])

    for b in range(blocks):
        load(0, b).start()
        load(1, b).start()
    for b in range(blocks):
        for k in (2, 3, 4):
            load(k, b).start()
    cap_copy = pltpu.make_async_copy(mid_cap.at[half], cap, cap_sem.at[0])
    tcap_copy = pltpu.make_async_copy(
        top_cap.at[0, ds(half * rank, rank)], tcap, cap_sem.at[1]
    )
    cap_copy.start()
    tcap_copy.start()

    barrier = pltpu.get_barrier_semaphore()
    peers = [partner, sibling, across] + [on_chip(d) for d in range(1, chips)]
    for peer in peers:
        pl.semaphore_signal(barrier, inc=1, device_id=(peer,), device_id_type=MESH)

    used = iter(range(send_sem.shape[0]))

    def send(src, dst, device):
        at = next(used)
        copy = pltpu.make_async_remote_copy(
            src_ref=src, dst_ref=dst, send_sem=send_sem.at[at], recv_sem=recv_sem.at[at],
            device_id=(device,), device_id_type=MESH,
        )
        copy.start()
        return copy

    def spread(view):
        return [send(view, view, on_chip(d)) for d in reversed(range(1, chips))]

    def wait(copies):
        for copy in copies:
            copy.wait()

    d_part[...] = jnp.zeros_like(d_part)

    def d_step(b, _):
        at = ds(b * leaf, leaf)
        load(0, b).wait()
        load(1, b).wait()
        v = split(vt[at, :])
        v_h[at, rank:], v_l[at, rank:] = v
        d_part[...] += dot3(split(ym[at, :].T), v, NN)
        return 0

    lax.fori_loop(0, blocks, d_step, 0)
    pl.semaphore_wait(barrier, len(peers))
    d_a = send(d_part.at[ds((1 - core) * hd, hd)], d_part_in, partner)

    def leaf_step(g, b):
        at = ds(b * leaf, leaf)
        here = slice(g * cols, (g + 1) * cols)
        if g == 0:
            for k in (2, 3, 4):
                load(k, b).wait()
            inv_h[at, :], inv_l[at, :] = split(inv[at, :])
            v_h[at, :rank], v_l[at, :rank] = split(vm[at, :])
        out = dot3((inv_h[at, :], inv_l[at, :]), split(rs[at, here]), NN)
        field[at, here] = out
        part[g] += dot3(split(out.T), (v_h[at, :], v_l[at, :]), NN)

    def leaf_run(g, first, last):
        def step(b, _):
            leaf_step(g, b)
            return 0

        lax.fori_loop(first, last, step, 0)

    def give_partner(g):
        return send(part.at[g, ds((1 - core) * hr, hr)], part_in.at[g], partner)

    def give_chips(g):
        chip_sum[g] = part[g, ds(core * hr, hr), :] + part_in[g]
        return [
            send(chip_sum.at[g, ds(flip(chip, d) * w, w)], chip_in.at[g, d], on_chip(d))
            for d in reversed(range(1, chips))
        ]

    def give_sibling(g):
        total = chip_sum[g, ds(chip * w, w), :]
        for d in range(1, chips):
            total += chip_in[g, d]
        pair[g, side] = total
        return send(pair.at[g, side], pair.at[g, side], sibling)

    def own(g):
        return ds(g * cols + (core * chips + chip) * w, w)

    def core_rows(g):
        return ds(g * cols + core * hr, hr)

    part[...] = jnp.zeros_like(part)
    leaf_run(0, 0, blocks)
    a0 = give_partner(0)
    d_a.wait()
    d_sum[...] = d_part[ds(core * hd, hd), :] + d_part_in[...]
    d_b = [
        send(d_sum.at[ds(flip(chip, d) * wd, wd)], d_in.at[d], on_chip(d))
        for d in reversed(range(1, chips))
    ]
    leaf_run(1, 0, blocks // 2)
    a0.wait()
    b0 = give_chips(0)
    wait(d_b)
    d_total = d_sum[ds(chip * wd, wd), :]
    for d in range(1, chips):
        d_total += d_in[d]
    d_own = ds((core * chips + chip) * wd, wd)
    d_full[side, d_own, :] = d_total
    d_z = send(d_full.at[side, d_own], d_full.at[side, d_own], sibling)
    leaf_run(1, blocks // 2, blocks)
    a1 = give_partner(1)
    field_copy = pltpu.make_async_copy(field, field_out, out_sem.at[0])
    field_copy.start()
    wait(b0)
    c0 = give_sibling(0)
    d_z.wait()
    d_ag = spread(d_full.at[:, d_own])
    a1.wait()
    b1 = give_chips(1)
    cap_copy.wait()
    tcap_copy.wait()
    cap_h[...], cap_l[...] = split(cap[...])
    tcap_h[...], tcap_l[...] = split(tcap[...])

    def middle(g):
        stacked = jnp.concatenate([pair[g, 1, :, :rank], pair[g, 0, :, :rank]], axis=1)
        both = dot3(split(stacked), (cap_h[...], cap_l[...]), NT)
        coef[own(g), :rank] = jnp.where(side == 0, both[:, :rank], both[:, rank:])
        return both, spread(coef.at[own(g), pl.ds(0, rank)])

    def give_across(g, both):
        total = pair[g, 0, :, rank:] + pair[g, 1, :, rank:]
        total -= dot3(split(both), (d_h[...], d_l[...]), NN)
        top_p[g, half] = total
        return send(top_p.at[g, half], top_p.at[g, half], across)

    def top(g):
        stacked = jnp.concatenate([top_p[g, 1], top_p[g, 0]], axis=1)
        coef[own(g), rank:] = dot3(split(stacked), (tcap_h[...], tcap_l[...]), NT)
        return spread(coef.at[own(g), pl.ds(rank, rank)])

    def forward(g, first):
        view = coef.at[core_rows(g), pl.ds(first, rank)]
        return send(view, view, partner)

    c0.wait()
    both0, mid0 = middle(0)
    wait(d_ag)
    d_half = d_full.at[:, ds(core * hd, hd)]
    d_f = send(d_half, d_half, partner)
    wait(b1)
    c1 = give_sibling(1)
    d_f.wait()
    for s in range(2):
        d_h[s * rank : (s + 1) * rank, :], d_l[s * rank : (s + 1) * rank, :] = split(d_full[s])
    x0 = give_across(0, both0)
    c1.wait()
    both1, mid1 = middle(1)
    x1 = give_across(1, both1)
    x0.wait()
    top0 = top(0)
    wait(mid0)
    f0 = forward(0, 0)
    x1.wait()
    top1 = top(1)
    wait(mid1)
    f1 = forward(1, 0)
    wait(top0)
    f2 = forward(0, rank)
    wait(top1)
    f3 = forward(1, rank)
    wait([f0, f1, f2, f3])
    coef_copy = pltpu.make_async_copy(coef, coef_out, out_sem.at[1])
    coef_copy.start()
    coef_copy.wait()
    field_copy.wait()


def coefficients(n, rs, inv, vm, ym, mid_cap, vt, top_cap):
    rows, rhs = rs.shape
    leaf = inv.shape[1]
    rank = vm.shape[1]
    m = n // 4
    chips = m // 2
    cols = rhs // GROUPS
    w, wd = cols // m, rank // m
    blocks = rows // leaf
    f32, bf16 = jnp.float32, jnp.bfloat16
    copies = 2 * chips + 2 + GROUPS * (3 * chips + 2)

    def vmem(*shape, dtype=f32):
        return pltpu.VMEM(shape, dtype)

    return pl.pallas_call(
        functools.partial(coef_kernel, n, leaf, rank),
        out_shape=(
            jax.ShapeDtypeStruct((rows, rhs), f32),
            jax.ShapeDtypeStruct((rhs, 2 * rank), f32),
        ),
        in_specs=[pl.BlockSpec(memory_space=pl.ANY)] * 7,
        out_specs=[pl.BlockSpec(memory_space=pl.ANY)] * 2,
        scratch_shapes=[
            vmem(rows, rhs), vmem(rows, leaf), vmem(rows, rank), vmem(rows, rank),
            vmem(rows, rank), vmem(2 * rank, 2 * rank), vmem(rank, 2 * rank), vmem(rows, rhs),
            vmem(rows, leaf, dtype=bf16), vmem(rows, leaf, dtype=bf16),
            vmem(rows, 2 * rank, dtype=bf16), vmem(rows, 2 * rank, dtype=bf16),
            vmem(2 * rank, 2 * rank, dtype=bf16), vmem(2 * rank, 2 * rank, dtype=bf16),
            vmem(rank, 2 * rank, dtype=bf16), vmem(rank, 2 * rank, dtype=bf16),
            vmem(2 * rank, rank, dtype=bf16), vmem(2 * rank, rank, dtype=bf16),
            vmem(GROUPS, cols, 2 * rank), vmem(GROUPS, cols // 2, 2 * rank),
            vmem(GROUPS, cols // 2, 2 * rank), vmem(GROUPS, chips, w, 2 * rank),
            vmem(GROUPS, 2, w, 2 * rank), vmem(GROUPS, 2, w, rank), vmem(rhs, 2 * rank),
            vmem(rank, rank), vmem(rank // 2, rank), vmem(rank // 2, rank),
            vmem(chips, wd, rank), vmem(2, rank, rank),
            pltpu.SemaphoreType.DMA((5, blocks)),
            pltpu.SemaphoreType.DMA((2,)),
            pltpu.SemaphoreType.DMA((2,)),
            pltpu.SemaphoreType.DMA((copies,)),
            pltpu.SemaphoreType.DMA((copies,)),
        ],
        compiler_params=pltpu.CompilerParams(
            collective_id=0, has_side_effects=True, vmem_limit_bytes=48 * 2**20
        ),
        name="coefficients",
    )(rs, inv, vm, ym, mid_cap, vt, top_cap)


def correct_kernel(field, ym, yt, coef, out, coef_h, coef_l):
    rank = ym.shape[1]

    @pl.when(pl.program_id(0) == 0)
    def _():
        coef_h[...], coef_l[...] = split(coef[...])

    fixing = dot3(split(ym[...]), (coef_h[:, :rank], coef_l[:, :rank]), NT)
    fixing += dot3(split(yt[...]), (coef_h[:, rank:], coef_l[:, rank:]), NT)
    out[...] = field[...] - fixing


def correct(field, ym, yt, coef):
    rows, rhs = field.shape
    rank = ym.shape[1]
    tile = 512
    return pl.pallas_call(
        correct_kernel,
        out_shape=jax.ShapeDtypeStruct((rows, rhs), jnp.float32),
        grid=(rows // tile,),
        in_specs=[
            pl.BlockSpec((tile, rhs), lambda i: (i, 0)),
            pl.BlockSpec((tile, rank), lambda i: (i, 0)),
            pl.BlockSpec((tile, rank), lambda i: (i, 0)),
            pl.BlockSpec((rhs, 2 * rank), lambda i: (0, 0)),
        ],
        out_specs=pl.BlockSpec((tile, rhs), lambda i: (i, 0)),
        scratch_shapes=[pltpu.VMEM((rhs, 2 * rank), jnp.bfloat16)] * 2,
        compiler_params=pltpu.CompilerParams(vmem_limit_bytes=32 * 2**20),
        name="correct",
    )(field, ym, yt, coef)


def per_device(
    n, right_sides, leaf_inverse, mid_proj, mid_basis, mid_cap, top_proj, top_basis, top_cap
):
    field, coef = coefficients(
        n, right_sides, leaf_inverse, mid_proj, mid_basis, mid_cap, top_proj, top_cap
    )
    return correct(field, mid_basis, top_basis, coef)


def solution(mesh):
    placed = (
        P("rows", None),
        P("rows", None),
        P("rows", None),
        P("rows", None),
        P(),
        P("rows", None),
        P("rows", None),
        P(),
    )
    return jax.shard_map(
        functools.partial(per_device, mesh.shape["rows"]),
        mesh=mesh,
        in_specs=placed,
        out_specs=P("rows", None),
        check_vma=False,
    )
```

```python
import functools

import jax
import jax.numpy as jnp
from jax import lax
from jax.experimental import pallas as pl
from jax.experimental.pallas import tpu as pltpu
from jax.sharding import PartitionSpec as P

MESH = pl.DeviceIdType.MESH
GROUPS = 2
NN = (((1,), (0,)), ((), ()))
NT = (((1,), (1,)), ((), ()))


def split(value):
    high = value.astype(jnp.bfloat16)
    return high, (value - high.astype(jnp.float32)).astype(jnp.bfloat16)


def dot3(left, right, dims):
    def one(a, b):
        return lax.dot_general(a, b, dims, preferred_element_type=jnp.float32)

    return one(left[0], right[0]) + (one(left[0], right[1]) + one(left[1], right[0]))


def flip(number, mask):
    bit = 1
    while bit <= mask:
        if mask & bit:
            number = number + (1 - 2 * (number // bit % 2)) * bit
        bit *= 2
    return number


def coef_kernel(
    n, leaf, rank,
    rs_hbm, inv_hbm, vm_hbm, ym_hbm, mid_cap, vt_hbm, yt_hbm, top_cap,
    field, coef_last,
    rs, inv, vm, vt, ym, yt, cap, tcap,
    inv_h, inv_l, v_h, v_l, cap_h, cap_l, tcap_h, tcap_l, d_h, d_l,
    part, part_in, chip_sum, chip_in, pair, top_p, coef,
    d_part, d_part_in, d_sum, d_in, d_full,
    load_sem, cap_sem, send_sem, recv_sem,
):
    m = n // 4
    chips = m // 2
    me = lax.axis_index("rows")
    quarter, place = me // m, me % m
    core, chip = place % 2, place // 2
    half, side = quarter // 2, quarter % 2
    partner = me + 1 - 2 * core
    sibling = me + m * (1 - 2 * side)
    across = me + 2 * m * (1 - 2 * half)
    rows, rhs = rs.shape
    blocks = rows // leaf
    cols = rhs // GROUPS
    hr = cols // 2
    w = cols // m
    wd = rank // m
    hd = rank // 2

    def on_chip(d):
        return me + 2 * (flip(chip, d) - chip)

    def ds(start, size):
        return pl.ds(pl.multiple_of(start, 8), size)

    loads = (
        (ym_hbm, ym), (vt_hbm, vt), (inv_hbm, inv), (rs_hbm, rs), (vm_hbm, vm), (yt_hbm, yt)
    )

    def load(k, b):
        src, dst = loads[k]
        at = ds(b * leaf, leaf)
        return pltpu.make_async_copy(src.at[at], dst.at[at], load_sem.at[k, b])

    def load_caps():
        return [
            pltpu.make_async_copy(mid_cap.at[half], cap, cap_sem.at[0]),
            pltpu.make_async_copy(top_cap.at[0, ds(half * rank, rank)], tcap, cap_sem.at[1]),
        ]

    def start(copies):
        for copy in copies:
            copy.start()

    def wait(copies):
        for copy in copies:
            copy.wait()

    start([load(k, b) for b in range(blocks) for k in (0, 1)])
    start([load(k, b) for b in range(blocks) for k in (2, 3, 4)])
    start(load_caps())
    start([load(5, b) for b in range(blocks)])

    barrier = pltpu.get_barrier_semaphore()
    peers = [partner, sibling, across] + [on_chip(d) for d in range(1, chips)]
    for peer in peers:
        pl.semaphore_signal(barrier, inc=1, device_id=(peer,), device_id_type=MESH)

    places = {}

    def remote(key, src, dst, device):
        at = places.setdefault(key, len(places))
        return pltpu.make_async_remote_copy(
            src_ref=src, dst_ref=dst, send_sem=send_sem.at[at], recv_sem=recv_sem.at[at],
            device_id=(device,), device_id_type=MESH,
        )

    others = tuple(reversed(range(1, chips)))

    def spread(key, view):
        return [remote((key, d), view, view, on_chip(d)) for d in others]

    def same(key, view, device):
        return [remote(key, view, view, device)]

    def d_own():
        return ds((core * chips + chip) * wd, wd)

    def d_core():
        return [remote("da", d_part.at[ds((1 - core) * hd, hd)], d_part_in, partner)]

    def d_chips():
        return [
            remote(("db", d), d_sum.at[ds(flip(chip, d) * wd, wd)], d_in.at[d], on_chip(d))
            for d in others
        ]

    def d_sibling():
        return same("dz", d_full.at[side, d_own()], sibling)

    def d_gather():
        return spread("dg", d_full.at[:, d_own()])

    def d_forward():
        return same("df", d_full.at[:, ds(core * hd, hd)], partner)

    def d_one():
        wait(d_core())
        d_sum[...] = d_part[ds(core * hd, hd), :] + d_part_in[...]
        start(d_chips())

    def d_two():
        wait(d_chips())
        total = d_sum[ds(chip * wd, wd), :]
        for d in others:
            total += d_in[d]
        d_full[side, d_own(), :] = total
        start(d_sibling())

    def d_three():
        wait(d_sibling())
        start(d_gather())

    def d_four():
        wait(d_gather())
        start(d_forward())

    def d_five():
        wait(d_forward())
        for s in range(2):
            at = slice(s * rank, (s + 1) * rank)
            d_h[at, :], d_l[at, :] = split(d_full[s])

    def to_core(g):
        return [remote(("a", g), part.at[g, ds((1 - core) * hr, hr)], part_in.at[g], partner)]

    def to_chips(g):
        return [
            remote(
                ("b", g, d), chip_sum.at[g, ds(flip(chip, d) * w, w)], chip_in.at[g, d], on_chip(d)
            )
            for d in others
        ]

    def to_sibling(g):
        return same(("c", g), pair.at[g, side], sibling)

    def to_across(g):
        return same(("x", g), top_p.at[g, half], across)

    def own(g):
        return ds(g * cols + (core * chips + chip) * w, w)

    def gather(g, level):
        return spread(("g", g, level), coef.at[own(g), pl.ds(level * rank, rank)])

    def forward(g, level):
        view = coef.at[ds(g * cols + core * hr, hr), pl.ds(level * rank, rank)]
        return same(("f", g, level), view, partner)

    def add_core(g):
        wait(to_core(g))
        chip_sum[g] = part[g, ds(core * hr, hr), :] + part_in[g]
        start(to_chips(g))

    def add_chips(g):
        wait(to_chips(g))
        total = chip_sum[g, ds(chip * w, w), :]
        for d in others:
            total += chip_in[g, d]
        pair[g, side] = total
        start(to_sibling(g))

    def middle(g):
        wait(to_sibling(g))
        stacked = jnp.concatenate([pair[g, 1, :, :rank], pair[g, 0, :, :rank]], axis=1)
        both = dot3(split(stacked), (cap_h[...], cap_l[...]), NT)
        coef[own(g), :rank] = jnp.where(side == 0, both[:, :rank], both[:, rank:])
        return both

    def cross(g, both):
        total = pair[g, 0, :, rank:] + pair[g, 1, :, rank:]
        top_p[g, half] = total - dot3(split(both), (d_h[...], d_l[...]), NN)
        start(to_across(g))

    def top(g):
        wait(to_across(g))
        stacked = jnp.concatenate([top_p[g, 1], top_p[g, 0]], axis=1)
        coef[own(g), rank:] = dot3(split(stacked), (tcap_h[...], tcap_l[...]), NT)
        start(gather(g, 1))

    def pass_on(g, level):
        wait(gather(g, level))
        start(forward(g, level))

    def correct_group(g, level):
        wait(forward(g, level))
        here = slice(g * cols, (g + 1) * cols)
        factor = split(coef[here, level * rank : (level + 1) * rank])
        basis = (ym, yt)[level]

        def step(b, _):
            at = ds(b * leaf, leaf)
            field[at, here] -= dot3(split(basis[at, :]), factor, NT)
            return 0

        lax.fori_loop(0, blocks, step, 0)

    def leaf_run(g, hooks):
        here = slice(g * cols, (g + 1) * cols)

        def step(b, _):
            for when, hook in hooks:
                pl.when(b == when)(hook)
            at = ds(b * leaf, leaf)
            if g == 0:
                wait([load(k, b) for k in (2, 3, 4)])
                inv_h[at, :], inv_l[at, :] = split(inv[at, :])
                v_h[at, :rank], v_l[at, :rank] = split(vm[at, :])
            out = dot3((inv_h[at, :], inv_l[at, :]), split(rs[at, here]), NN)
            field[at, here] = out
            part[g] += dot3(split(out.T), (v_h[at, :], v_l[at, :]), NN)
            return 0

        lax.fori_loop(0, blocks, step, 0)

    def split_caps():
        wait(load_caps())
        cap_h[...], cap_l[...] = split(cap[...])
        tcap_h[...], tcap_l[...] = split(tcap[...])

    d_part[...] = jnp.zeros_like(d_part)
    part[...] = jnp.zeros_like(part)

    def d_step(b, _):
        at = ds(b * leaf, leaf)
        wait([load(0, b), load(1, b)])
        v = split(vt[at, :])
        v_h[at, rank:], v_l[at, rank:] = v
        d_part[...] += dot3(split(ym[at, :].T), v, NN)
        return 0

    lax.fori_loop(0, blocks, d_step, 0)
    pl.semaphore_wait(barrier, len(peers))
    start(d_core())
    leaf_run(0, ((1, d_one), (blocks - 1, d_two)))
    start(to_core(0))
    d_three()
    leaf_run(1, ((1, lambda: add_core(0)), (2, d_four), (blocks - 1, lambda: add_chips(0))))
    start(to_core(1))
    split_caps()
    add_core(1)
    both = middle(0)
    start(gather(0, 0))
    d_five()
    cross(0, both)
    add_chips(1)
    top(0)
    both = middle(1)
    cross(1, both)
    start(gather(1, 0))
    pass_on(0, 0)
    wait([load(5, b) for b in range(blocks)])
    correct_group(0, 0)
    top(1)
    pass_on(0, 1)
    pass_on(1, 0)
    correct_group(0, 1)
    pass_on(1, 1)
    correct_group(1, 0)
    wait(forward(1, 1))
    coef_last[...] = coef[cols:, rank:]


def coefficients(n, rs, inv, vm, ym, mid_cap, vt, yt, top_cap):
    rows, rhs = rs.shape
    leaf = inv.shape[1]
    rank = vm.shape[1]
    m = n // 4
    chips = m // 2
    cols = rhs // GROUPS
    w, wd = cols // m, rank // m
    blocks = rows // leaf
    f32, bf16 = jnp.float32, jnp.bfloat16
    copies = 2 * chips + 2 + GROUPS * (3 * chips + 2)

    def vmem(*shape, dtype=f32):
        return pltpu.VMEM(shape, dtype)

    return pl.pallas_call(
        functools.partial(coef_kernel, n, leaf, rank),
        out_shape=(vmem(rows, rhs), vmem(cols, rank)),
        in_specs=[pl.BlockSpec(memory_space=pltpu.HBM)] * 8,
        out_specs=[pl.BlockSpec(memory_space=pltpu.VMEM)] * 2,
        scratch_shapes=[
            vmem(rows, rhs), vmem(rows, leaf), vmem(rows, rank), vmem(rows, rank),
            vmem(rows, rank), vmem(rows, rank), vmem(2 * rank, 2 * rank), vmem(rank, 2 * rank),
            vmem(rows, leaf, dtype=bf16), vmem(rows, leaf, dtype=bf16),
            vmem(rows, 2 * rank, dtype=bf16), vmem(rows, 2 * rank, dtype=bf16),
            vmem(2 * rank, 2 * rank, dtype=bf16), vmem(2 * rank, 2 * rank, dtype=bf16),
            vmem(rank, 2 * rank, dtype=bf16), vmem(rank, 2 * rank, dtype=bf16),
            vmem(2 * rank, rank, dtype=bf16), vmem(2 * rank, rank, dtype=bf16),
            vmem(GROUPS, cols, 2 * rank), vmem(GROUPS, cols // 2, 2 * rank),
            vmem(GROUPS, cols // 2, 2 * rank), vmem(GROUPS, chips, w, 2 * rank),
            vmem(GROUPS, 2, w, 2 * rank), vmem(GROUPS, 2, w, rank), vmem(rhs, 2 * rank),
            vmem(rank, rank), vmem(rank // 2, rank), vmem(rank // 2, rank),
            vmem(chips, wd, rank), vmem(2, rank, rank),
            pltpu.SemaphoreType.DMA((6, blocks)),
            pltpu.SemaphoreType.DMA((2,)),
            pltpu.SemaphoreType.DMA((copies,)),
            pltpu.SemaphoreType.DMA((copies,)),
        ],
        compiler_params=pltpu.CompilerParams(
            collective_id=0, has_side_effects=True, vmem_limit_bytes=44 * 2**20
        ),
        name="coefficients",
    )(rs, inv, vm, ym, mid_cap, vt, yt, top_cap)


def finish_kernel(field, yt, coef, out, last, sem):
    rows, rhs = out.shape
    cols = coef.shape[0]
    done = rhs - cols
    tile = rows // 4
    left = pltpu.make_async_copy(
        field.at[:, pl.ds(0, done)], out.at[:, pl.ds(0, done)], sem.at[4]
    )
    left.start()
    factor = split(coef[...])
    copies = []
    for i in range(4):
        at = slice(i * tile, (i + 1) * tile)
        last[at, :] = field[at, done:] - dot3(split(yt[at, :]), factor, NT)
        copy = pltpu.make_async_copy(
            last.at[pl.ds(i * tile, tile)],
            out.at[pl.ds(i * tile, tile), pl.ds(done, cols)],
            sem.at[i],
        )
        copy.start()
        copies.append(copy)
    left.wait()
    for copy in copies:
        copy.wait()


def finish(field, yt, coef):
    rows, rhs = field.shape
    return pl.pallas_call(
        finish_kernel,
        out_shape=jax.ShapeDtypeStruct((rows, rhs), jnp.float32),
        in_specs=[pl.BlockSpec(memory_space=pltpu.VMEM)] * 3,
        out_specs=pl.BlockSpec(memory_space=pltpu.HBM),
        scratch_shapes=[
            pltpu.VMEM((rows, coef.shape[0]), jnp.float32),
            pltpu.SemaphoreType.DMA((5,)),
        ],
        compiler_params=pltpu.CompilerParams(vmem_limit_bytes=16 * 2**20),
        name="finish",
    )(field, yt, coef)


def per_device(
    n, right_sides, leaf_inverse, mid_proj, mid_basis, mid_cap, top_proj, top_basis, top_cap
):
    field, coef = coefficients(
        n, right_sides, leaf_inverse, mid_proj, mid_basis, mid_cap, top_proj, top_basis, top_cap
    )
    return finish(field, top_basis, coef)


def solution(mesh):
    placed = (
        P("rows", None),
        P("rows", None),
        P("rows", None),
        P("rows", None),
        P(),
        P("rows", None),
        P("rows", None),
        P(),
    )
    return jax.shard_map(
        functools.partial(per_device, mesh.shape["rows"]),
        mesh=mesh,
        in_specs=placed,
        out_specs=P("rows", None),
        check_vma=False,
    )
```

```python
import functools

import jax
import jax.numpy as jnp
from jax import lax
from jax.experimental import pallas as pl
from jax.experimental.pallas import tpu as pltpu
from jax.sharding import PartitionSpec as P

MESH = pl.DeviceIdType.MESH
GROUPS = 2
NN = (((1,), (0,)), ((), ()))
NT = (((1,), (1,)), ((), ()))


def split(value):
    high = value.astype(jnp.bfloat16)
    return high, (value - high.astype(jnp.float32)).astype(jnp.bfloat16)


def left3(value, axis=1):
    high, low = split(value)
    return jnp.concatenate([high, high, low], axis=axis)


def right3(value, axis):
    high, low = split(value)
    return jnp.concatenate([high, low, high], axis=axis)


def dot(left, right, dims):
    return lax.dot_general(left, right, dims, preferred_element_type=jnp.float32)


def flip(number, mask):
    bit = 1
    while bit <= mask:
        if mask & bit:
            number = number + (1 - 2 * (number // bit % 2)) * bit
        bit *= 2
    return number


def coef_kernel(
    n, leaf, rank,
    rs_hbm, inv_hbm, vm_hbm, ym_hbm, mid_cap, vt_hbm, yt_hbm, top_cap,
    field, coef_last,
    rs, inv, vm, vt, ym, yt, cap, tcap,
    inv3, v3, cap3, tcap3, d3,
    proj, part, part_in, chip_sum, chip_in, pair, top_p, coef,
    d_part, d_part_in, d_sum, d_in, d_full,
    load_sem, cap_sem, send_sem, recv_sem,
):
    m = n // 4
    chips = m // 2
    me = lax.axis_index("rows")
    quarter, place = me // m, me % m
    core, chip = place % 2, place // 2
    half, side = quarter // 2, quarter % 2
    partner = me + 1 - 2 * core
    sibling = me + m * (1 - 2 * side)
    across = me + 2 * m * (1 - 2 * half)
    rows, rhs = rs.shape
    blocks = rows // leaf
    cols = rhs // GROUPS
    hr = cols // 2
    w = cols // m
    wd = rank // m
    hd = rank // 2

    def on_chip(d):
        return me + 2 * (flip(chip, d) - chip)

    def ds(start, size):
        return pl.ds(pl.multiple_of(start, 8), size)

    loads = (
        (ym_hbm, ym), (vt_hbm, vt), (inv_hbm, inv), (rs_hbm, rs), (vm_hbm, vm), (yt_hbm, yt)
    )

    def load(k, b):
        src, dst = loads[k]
        at = ds(b * leaf, leaf)
        return pltpu.make_async_copy(src.at[at], dst.at[at], load_sem.at[k, b])

    def load_caps():
        return [
            pltpu.make_async_copy(mid_cap.at[half], cap, cap_sem.at[0]),
            pltpu.make_async_copy(top_cap.at[0, ds(half * rank, rank)], tcap, cap_sem.at[1]),
        ]

    def start(copies):
        for copy in copies:
            copy.start()

    def wait(copies):
        for copy in copies:
            copy.wait()

    start([load(k, b) for b in range(blocks) for k in (0, 1)])
    start([load(k, b) for b in range(blocks) for k in (2, 3, 4)])
    start(load_caps())
    start([load(5, b) for b in range(blocks)])

    barrier = pltpu.get_barrier_semaphore()
    peers = [partner, sibling, across] + [on_chip(d) for d in range(1, chips)]
    for peer in peers:
        pl.semaphore_signal(barrier, inc=1, device_id=(peer,), device_id_type=MESH)

    places = {}

    def remote(key, src, dst, device):
        at = places.setdefault(key, len(places))
        return pltpu.make_async_remote_copy(
            src_ref=src, dst_ref=dst, send_sem=send_sem.at[at], recv_sem=recv_sem.at[at],
            device_id=(device,), device_id_type=MESH,
        )

    others = tuple(reversed(range(1, chips)))

    def spread(key, view):
        return [remote((key, d), view, view, on_chip(d)) for d in others]

    def same(key, view, device):
        return [remote(key, view, view, device)]

    def d_own():
        return ds((core * chips + chip) * wd, wd)

    def d_core():
        return [remote("da", d_part.at[ds((1 - core) * hd, hd)], d_part_in, partner)]

    def d_chips():
        return [
            remote(("db", d), d_sum.at[ds(flip(chip, d) * wd, wd)], d_in.at[d], on_chip(d))
            for d in others
        ]

    def d_sibling():
        return same("dz", d_full.at[side, d_own()], sibling)

    def d_gather():
        return spread("dg", d_full.at[:, d_own()])

    def d_forward():
        return same("df", d_full.at[:, ds(core * hd, hd)], partner)

    def d_one():
        wait(d_core())
        d_sum[...] = d_part[ds(core * hd, hd), :] + d_part_in[...]
        start(d_chips())

    def d_two():
        wait(d_chips())
        total = d_sum[ds(chip * wd, wd), :]
        for d in others:
            total += d_in[d]
        d_full[side, d_own(), :] = total
        start(d_sibling())

    def d_three():
        wait(d_sibling())
        start(d_gather())

    def d_four():
        wait(d_gather())
        start(d_forward())

    def d_five():
        wait(d_forward())
        d3[...] = right3(jnp.concatenate([d_full[0], d_full[1]], axis=1), 1)

    def to_core(g):
        return [remote(("a", g), part.at[g, ds((1 - core) * hr, hr)], part_in.at[g], partner)]

    def to_chips(g):
        return [
            remote(
                ("b", g, d), chip_sum.at[g, ds(flip(chip, d) * w, w)], chip_in.at[g, d], on_chip(d)
            )
            for d in others
        ]

    def to_sibling(g):
        return same(("c", g), pair.at[g, side], sibling)

    def to_across(g):
        return same(("x", g), top_p.at[g, half], across)

    def own(g):
        return ds(g * cols + (core * chips + chip) * w, w)

    def gather(g, level):
        return spread(("g", g, level), coef.at[own(g), pl.ds(level * rank, rank)])

    def forward(g, level):
        view = coef.at[ds(g * cols + core * hr, hr), pl.ds(level * rank, rank)]
        return same(("f", g, level), view, partner)

    def add_core(g):
        wait(to_core(g))
        chip_sum[g] = part[g, ds(core * hr, hr), :] + part_in[g]
        start(to_chips(g))

    def add_chips(g):
        wait(to_chips(g))
        total = chip_sum[g, ds(chip * w, w), :]
        for d in others:
            total += chip_in[g, d]
        pair[g, side] = total
        start(to_sibling(g))

    def middle(g):
        wait(to_sibling(g))
        stacked = jnp.concatenate([pair[g, 1, :, :rank], pair[g, 0, :, :rank]], axis=1)
        both = dot(left3(stacked), cap3[...], NT)
        coef[own(g), :rank] = jnp.where(side == 0, both[:, :rank], both[:, rank:])
        return both

    def cross(g, both):
        total = pair[g, 0, :, rank:] + pair[g, 1, :, rank:]
        top_p[g, half] = total - dot(left3(both), d3[...], NT)
        start(to_across(g))

    def top(g):
        wait(to_across(g))
        stacked = jnp.concatenate([top_p[g, 1], top_p[g, 0]], axis=1)
        coef[own(g), rank:] = dot(left3(stacked), tcap3[...], NT)
        start(gather(g, 1))

    def pass_on(g, level):
        wait(gather(g, level))
        start(forward(g, level))

    def correct_group(g, level):
        wait(forward(g, level))
        here = slice(g * cols, (g + 1) * cols)
        factor = right3(coef[here, level * rank : (level + 1) * rank], 1)
        basis = (ym, yt)[level]

        def step(b, _):
            at = ds(b * leaf, leaf)
            field[at, here] -= dot(left3(basis[at, :]), factor, NT)
            return 0

        lax.fori_loop(0, blocks, step, 0)

    def leaf_run(g, hooks):
        here = slice(g * cols, (g + 1) * cols)

        def step(i, _):
            for when, hook in hooks:
                pl.when(i == when)(hook)
            outs = []
            for b in (2 * i, 2 * i + 1):
                at = ds(b * leaf, leaf)
                if g == 0:
                    wait([load(k, b) for k in (2, 3, 4)])
                    inv3[at, :] = left3(inv[at, :])
                    v3[b, :rank, :] = left3(vm[at, :].T)
                out = dot(inv3[at, :], right3(rs[at, here], 0), NN)
                field[at, here] = out
                outs.append(right3(out, 0))
            proj[...] += dot(v3[2 * i], outs[0], NN) + dot(v3[2 * i + 1], outs[1], NN)
            return 0

        proj[...] = jnp.zeros_like(proj)
        lax.fori_loop(0, blocks // 2, step, 0)
        part[g] = proj[...].T

    def split_caps():
        wait(load_caps())
        cap3[...] = right3(cap[...], 1)
        tcap3[...] = right3(tcap[...], 1)

    d_part[...] = jnp.zeros_like(d_part)

    def d_step(b, _):
        at = ds(b * leaf, leaf)
        wait([load(0, b), load(1, b)])
        v = left3(vt[at, :].T)
        v3[b, rank:, :] = v
        d_part[...] += dot(v, right3(ym[at, :], 0), NN)
        return 0

    lax.fori_loop(0, blocks, d_step, 0)
    pl.semaphore_wait(barrier, len(peers))
    start(d_core())
    leaf_run(0, ((1, d_one),))
    start(to_core(0))
    d_two()
    split_caps()

    def between():
        add_core(0)
        d_three()

    leaf_run(1, ((1, between),))
    start(to_core(1))
    add_chips(0)
    d_four()
    add_core(1)
    both = middle(0)
    start(gather(0, 0))
    d_five()
    cross(0, both)
    add_chips(1)
    top(0)
    both = middle(1)
    cross(1, both)
    start(gather(1, 0))
    pass_on(0, 0)
    wait([load(5, b) for b in range(blocks)])
    correct_group(0, 0)
    top(1)
    pass_on(0, 1)
    pass_on(1, 0)
    correct_group(0, 1)
    pass_on(1, 1)
    correct_group(1, 0)
    wait(forward(1, 1))
    coef_last[...] = coef[cols:, rank:]


def coefficients(n, rs, inv, vm, ym, mid_cap, vt, yt, top_cap):
    rows, rhs = rs.shape
    leaf = inv.shape[1]
    rank = vm.shape[1]
    m = n // 4
    chips = m // 2
    cols = rhs // GROUPS
    w, wd = cols // m, rank // m
    blocks = rows // leaf
    f32, bf16 = jnp.float32, jnp.bfloat16
    copies = 2 * chips + 2 + GROUPS * (3 * chips + 2)

    def vmem(*shape, dtype=f32):
        return pltpu.VMEM(shape, dtype)

    return pl.pallas_call(
        functools.partial(coef_kernel, n, leaf, rank),
        out_shape=(vmem(rows, rhs), vmem(cols, rank)),
        in_specs=[pl.BlockSpec(memory_space=pltpu.HBM)] * 8,
        out_specs=[pl.BlockSpec(memory_space=pltpu.VMEM)] * 2,
        scratch_shapes=[
            vmem(rows, rhs), vmem(rows, leaf), vmem(rows, rank), vmem(rows, rank),
            vmem(rows, rank), vmem(rows, rank), vmem(2 * rank, 2 * rank), vmem(rank, 2 * rank),
            vmem(rows, 3 * leaf, dtype=bf16), vmem(blocks, 2 * rank, 3 * leaf, dtype=bf16),
            vmem(2 * rank, 6 * rank, dtype=bf16), vmem(rank, 6 * rank, dtype=bf16),
            vmem(rank, 6 * rank, dtype=bf16), vmem(2 * rank, cols),
            vmem(GROUPS, cols, 2 * rank), vmem(GROUPS, cols // 2, 2 * rank),
            vmem(GROUPS, cols // 2, 2 * rank), vmem(GROUPS, chips, w, 2 * rank),
            vmem(GROUPS, 2, w, 2 * rank), vmem(GROUPS, 2, w, rank), vmem(rhs, 2 * rank),
            vmem(rank, rank), vmem(rank // 2, rank), vmem(rank // 2, rank),
            vmem(chips, wd, rank), vmem(2, rank, rank),
            pltpu.SemaphoreType.DMA((6, blocks)),
            pltpu.SemaphoreType.DMA((2,)),
            pltpu.SemaphoreType.DMA((copies,)),
            pltpu.SemaphoreType.DMA((copies,)),
        ],
        compiler_params=pltpu.CompilerParams(
            collective_id=0, has_side_effects=True, vmem_limit_bytes=56 * 2**20
        ),
        name="coefficients",
    )(rs, inv, vm, ym, mid_cap, vt, yt, top_cap)


def finish_kernel(field, yt, coef, out, last, sem):
    rows, rhs = out.shape
    cols = coef.shape[0]
    done = rhs - cols
    tile = rows // 4
    left = pltpu.make_async_copy(
        field.at[:, pl.ds(0, done)], out.at[:, pl.ds(0, done)], sem.at[4]
    )
    left.start()
    factor = right3(coef[...], 1)
    copies = []
    for i in range(4):
        at = slice(i * tile, (i + 1) * tile)
        last[at, :] = field[at, done:] - dot(left3(yt[at, :]), factor, NT)
        copy = pltpu.make_async_copy(
            last.at[pl.ds(i * tile, tile)],
            out.at[pl.ds(i * tile, tile), pl.ds(done, cols)],
            sem.at[i],
        )
        copy.start()
        copies.append(copy)
    left.wait()
    for copy in copies:
        copy.wait()


def finish(field, yt, coef):
    rows, rhs = field.shape
    return pl.pallas_call(
        finish_kernel,
        out_shape=jax.ShapeDtypeStruct((rows, rhs), jnp.float32),
        in_specs=[pl.BlockSpec(memory_space=pltpu.VMEM)] * 3,
        out_specs=pl.BlockSpec(memory_space=pltpu.HBM),
        scratch_shapes=[
            pltpu.VMEM((rows, coef.shape[0]), jnp.float32),
            pltpu.SemaphoreType.DMA((5,)),
        ],
        compiler_params=pltpu.CompilerParams(vmem_limit_bytes=16 * 2**20),
        name="finish",
    )(field, yt, coef)


def per_device(
    n, right_sides, leaf_inverse, mid_proj, mid_basis, mid_cap, top_proj, top_basis, top_cap
):
    field, coef = coefficients(
        n, right_sides, leaf_inverse, mid_proj, mid_basis, mid_cap, top_proj, top_basis, top_cap
    )
    return finish(field, top_basis, coef)


def solution(mesh):
    placed = (
        P("rows", None),
        P("rows", None),
        P("rows", None),
        P("rows", None),
        P(),
        P("rows", None),
        P("rows", None),
        P(),
    )
    return jax.shard_map(
        functools.partial(per_device, mesh.shape["rows"]),
        mesh=mesh,
        in_specs=placed,
        out_specs=P("rows", None),
        check_vma=False,
    )
```

```python
import functools

import jax
import jax.numpy as jnp
from jax import lax
from jax.experimental import pallas as pl
from jax.experimental.pallas import tpu as pltpu
from jax.sharding import PartitionSpec as P

MESH = pl.DeviceIdType.MESH
GROUPS = 2
NN = (((1,), (0,)), ((), ()))
NT = (((1,), (1,)), ((), ()))


def split(value):
    high = value.astype(jnp.bfloat16)
    return high, (value - high.astype(jnp.float32)).astype(jnp.bfloat16)


def both_parts(value):
    high, low = split(value)
    return jnp.stack([high, low])


def small_dot(value, parts, dims):
    count = value.shape[0]
    high = value.astype(jnp.bfloat16).astype(jnp.float32)
    stacked = jnp.concatenate([high, value - high], axis=0).astype(jnp.bfloat16)
    wide = dot(stacked, parts[0], dims)
    return wide[:count] + (wide[count:] + dot(high.astype(jnp.bfloat16), parts[1], dims))


def left3(value, axis=1):
    high, low = split(value)
    return jnp.concatenate([high, high, low], axis=axis)


def right3(value, axis):
    high, low = split(value)
    return jnp.concatenate([high, low, high], axis=axis)


def dot(left, right, dims):
    return lax.dot_general(left, right, dims, preferred_element_type=jnp.float32)


def flip(number, mask):
    bit = 1
    while bit <= mask:
        if mask & bit:
            number = number + (1 - 2 * (number // bit % 2)) * bit
        bit *= 2
    return number


def coef_kernel(
    n, leaf, rank,
    rs_hbm, inv_hbm, vm_hbm, ym_hbm, mid_cap, vt_hbm, yt_hbm, top_cap,
    field, yt, coef_last,
    rs, inv, vm, vt, ym, cap, tcap,
    inv3, v3, cap2, tcap2, d2,
    proj, part, part_in, chip_sum, chip_in, pair, top_p, coef,
    d_part, d_part_in, d_sum, d_in, d_full,
    load_sem, cap_sem, send_sem, recv_sem,
):
    m = n // 4
    chips = m // 2
    me = lax.axis_index("rows")
    quarter, place = me // m, me % m
    core, chip = place % 2, place // 2
    half, side = quarter // 2, quarter % 2
    partner = me + 1 - 2 * core
    sibling = me + m * (1 - 2 * side)
    across = me + 2 * m * (1 - 2 * half)
    rows, rhs = rs.shape
    blocks = rows // leaf
    cols = rhs // GROUPS
    hr = cols // 2
    w = cols // m
    wd = rank // m
    hd = rank // 2

    def on_chip(d):
        return me + 2 * (flip(chip, d) - chip)

    def ds(start, size):
        return pl.ds(pl.multiple_of(start, 8), size)

    loads = (
        (ym_hbm, ym), (vt_hbm, vt), (inv_hbm, inv), (vm_hbm, vm), (yt_hbm, yt), (rs_hbm, rs)
    )

    def load(k, b):
        src, dst = loads[k]
        at = ds(b * leaf, leaf)
        return pltpu.make_async_copy(src.at[at], dst.at[at], load_sem.at[k, b])

    def load_rs(g, b):
        at = (ds(b * leaf, leaf), pl.ds(g * cols, cols))
        return pltpu.make_async_copy(rs_hbm.at[at], rs.at[at], load_sem.at[5 + g, b])

    def load_caps():
        return [
            pltpu.make_async_copy(mid_cap.at[half], cap, cap_sem.at[0]),
            pltpu.make_async_copy(top_cap.at[0, ds(half * rank, rank)], tcap, cap_sem.at[1]),
        ]

    def start(copies):
        for copy in copies:
            copy.start()

    def wait(copies):
        for copy in copies:
            copy.wait()

    start([load(k, b) for b in range(blocks) for k in (0, 1)])
    for b in range(blocks):
        start([load(2, b), load_rs(0, b), load(3, b)])
    start([load_rs(1, b) for b in range(blocks)])
    start(load_caps())
    start([load(4, b) for b in range(blocks)])

    barrier = pltpu.get_barrier_semaphore()
    peers = [partner, sibling, across] + [on_chip(d) for d in range(1, chips)]
    for peer in peers:
        pl.semaphore_signal(barrier, inc=1, device_id=(peer,), device_id_type=MESH)

    places = {}

    def remote(key, src, dst, device):
        at = places.setdefault(key, len(places))
        return pltpu.make_async_remote_copy(
            src_ref=src, dst_ref=dst, send_sem=send_sem.at[at], recv_sem=recv_sem.at[at],
            device_id=(device,), device_id_type=MESH,
        )

    others = tuple(reversed(range(1, chips)))

    def spread(key, view):
        return [remote((key, d), view, view, on_chip(d)) for d in others]

    def same(key, view, device):
        return [remote(key, view, view, device)]

    def d_own():
        return ds((core * chips + chip) * wd, wd)

    def d_core():
        return [remote("da", d_part.at[ds((1 - core) * hd, hd)], d_part_in, partner)]

    def d_chips():
        return [
            remote(("db", d), d_sum.at[ds(flip(chip, d) * wd, wd)], d_in.at[d], on_chip(d))
            for d in others
        ]

    def d_sibling():
        return same("dz", d_full.at[side, d_own()], sibling)

    def d_gather():
        return spread("dg", d_full.at[:, d_own()])

    def d_forward():
        return same("df", d_full.at[:, ds(core * hd, hd)], partner)

    def d_one():
        wait(d_core())
        d_sum[...] = d_part[ds(core * hd, hd), :] + d_part_in[...]
        start(d_chips())

    def d_two():
        wait(d_chips())
        total = d_sum[ds(chip * wd, wd), :]
        for d in others:
            total += d_in[d]
        d_full[side, d_own(), :] = total
        start(d_sibling())

    def d_three():
        wait(d_sibling())
        start(d_gather())

    def d_four():
        wait(d_gather())
        start(d_forward())

    def d_five():
        wait(d_forward())
        d2[...] = both_parts(jnp.concatenate([d_full[0], d_full[1]], axis=1))

    def to_core(g):
        return [remote(("a", g), part.at[g, ds((1 - core) * hr, hr)], part_in.at[g], partner)]

    def to_chips(g):
        return [
            remote(
                ("b", g, d), chip_sum.at[g, ds(flip(chip, d) * w, w)], chip_in.at[g, d], on_chip(d)
            )
            for d in others
        ]

    def to_sibling(g):
        return same(("c", g), pair.at[g, side], sibling)

    def to_across(g):
        return same(("x", g), top_p.at[g, half], across)

    def own(g):
        return ds(g * cols + (core * chips + chip) * w, w)

    def gather(g, level):
        return spread(("g", g, level), coef.at[own(g), pl.ds(level * rank, rank)])

    def forward(g, level):
        view = coef.at[ds(g * cols + core * hr, hr), pl.ds(level * rank, rank)]
        return same(("f", g, level), view, partner)

    def add_core(g):
        wait(to_core(g))
        chip_sum[g] = part[g, ds(core * hr, hr), :] + part_in[g]
        start(to_chips(g))

    def add_chips(g):
        wait(to_chips(g))
        total = chip_sum[g, ds(chip * w, w), :]
        for d in others:
            total += chip_in[g, d]
        pair[g, side] = total
        start(to_sibling(g))

    def middle(g):
        wait(to_sibling(g))
        stacked = jnp.concatenate([pair[g, 1, :, :rank], pair[g, 0, :, :rank]], axis=1)
        both = small_dot(stacked, cap2, NT)
        coef[own(g), :rank] = jnp.where(side == 0, both[:, :rank], both[:, rank:])
        return both

    def cross(g, both):
        total = pair[g, 0, :, rank:] + pair[g, 1, :, rank:]
        top_p[g, half] = total - small_dot(both, d2, NT)
        start(to_across(g))

    def top(g):
        wait(to_across(g))
        stacked = jnp.concatenate([top_p[g, 1], top_p[g, 0]], axis=1)
        coef[own(g), rank:] = small_dot(stacked, tcap2, NT)
        start(gather(g, 1))

    def pass_on(g, level):
        wait(gather(g, level))
        start(forward(g, level))

    def correct_group(g, level):
        wait(forward(g, level))
        here = slice(g * cols, (g + 1) * cols)
        factor = right3(coef[here, level * rank : (level + 1) * rank], 1)
        basis = (ym, yt)[level]

        def step(b, _):
            at = ds(b * leaf, leaf)
            field[at, here] -= dot(left3(basis[at, :]), factor, NT)
            return 0

        lax.fori_loop(0, blocks, step, 0)

    def leaf_run(g, hooks):
        here = slice(g * cols, (g + 1) * cols)

        def step(i, _):
            for when, hook in hooks:
                pl.when(i == when)(hook)
            outs = []
            for b in (2 * i, 2 * i + 1):
                at = ds(b * leaf, leaf)
                if g == 0:
                    wait([load(2, b), load(3, b)])
                    inv3[at, :] = left3(inv[at, :])
                    v3[b, :rank, :] = left3(vm[at, :].T)
                wait([load_rs(g, b)])
                out = dot(inv3[at, :], right3(rs[at, here], 0), NN)
                field[at, here] = out
                outs.append(right3(out, 0))
            proj[...] += dot(v3[2 * i], outs[0], NN) + dot(v3[2 * i + 1], outs[1], NN)
            return 0

        proj[...] = jnp.zeros_like(proj)
        lax.fori_loop(0, blocks // 2, step, 0)
        part[g] = proj[...].T

    def split_caps():
        wait(load_caps())
        cap2[...] = both_parts(cap[...])
        tcap2[...] = both_parts(tcap[...])

    d_part[...] = jnp.zeros_like(d_part)

    def d_step(b, _):
        at = ds(b * leaf, leaf)
        wait([load(0, b), load(1, b)])
        v = left3(vt[at, :].T)
        v3[b, rank:, :] = v
        d_part[...] += dot(v, right3(ym[at, :], 0), NN)
        return 0

    lax.fori_loop(0, blocks, d_step, 0)
    pl.semaphore_wait(barrier, len(peers))
    start(d_core())
    leaf_run(0, ((1, d_one),))
    start(to_core(0))
    d_two()
    split_caps()

    def between():
        add_core(0)
        d_three()

    leaf_run(1, ((1, between),))
    start(to_core(1))
    add_chips(0)
    d_four()
    add_core(1)
    both = middle(0)
    start(gather(0, 0))
    d_five()
    cross(0, both)
    add_chips(1)
    top(0)
    pass_on(0, 0)
    both = middle(1)
    cross(1, both)
    start(gather(1, 0))
    wait([load(4, b) for b in range(blocks)])
    correct_group(0, 0)
    top(1)
    pass_on(0, 1)
    pass_on(1, 0)
    correct_group(0, 1)
    pass_on(1, 1)
    correct_group(1, 0)
    wait(forward(1, 1))
    coef_last[...] = coef[cols:, rank:]


def coefficients(n, rs, inv, vm, ym, mid_cap, vt, yt, top_cap):
    rows, rhs = rs.shape
    leaf = inv.shape[1]
    rank = vm.shape[1]
    m = n // 4
    chips = m // 2
    cols = rhs // GROUPS
    w, wd = cols // m, rank // m
    blocks = rows // leaf
    f32, bf16 = jnp.float32, jnp.bfloat16
    copies = 2 * chips + 2 + GROUPS * (3 * chips + 2)

    def vmem(*shape, dtype=f32):
        return pltpu.VMEM(shape, dtype)

    return pl.pallas_call(
        functools.partial(coef_kernel, n, leaf, rank),
        out_shape=(vmem(rows, rhs), vmem(rows, rank), vmem(cols, rank)),
        in_specs=[pl.BlockSpec(memory_space=pltpu.HBM)] * 8,
        out_specs=[pl.BlockSpec(memory_space=pltpu.VMEM)] * 3,
        scratch_shapes=[
            vmem(rows, rhs), vmem(rows, leaf), vmem(rows, rank), vmem(rows, rank),
            vmem(rows, rank), vmem(2 * rank, 2 * rank), vmem(rank, 2 * rank),
            vmem(rows, 3 * leaf, dtype=bf16), vmem(blocks, 2 * rank, 3 * leaf, dtype=bf16),
            vmem(2, 2 * rank, 2 * rank, dtype=bf16), vmem(2, rank, 2 * rank, dtype=bf16),
            vmem(2, rank, 2 * rank, dtype=bf16), vmem(2 * rank, cols),
            vmem(GROUPS, cols, 2 * rank), vmem(GROUPS, cols // 2, 2 * rank),
            vmem(GROUPS, cols // 2, 2 * rank), vmem(GROUPS, chips, w, 2 * rank),
            vmem(GROUPS, 2, w, 2 * rank), vmem(GROUPS, 2, w, rank), vmem(rhs, 2 * rank),
            vmem(rank, rank), vmem(rank // 2, rank), vmem(rank // 2, rank),
            vmem(chips, wd, rank), vmem(2, rank, rank),
            pltpu.SemaphoreType.DMA((5 + GROUPS, blocks)),
            pltpu.SemaphoreType.DMA((2,)),
            pltpu.SemaphoreType.DMA((copies,)),
            pltpu.SemaphoreType.DMA((copies,)),
        ],
        compiler_params=pltpu.CompilerParams(
            collective_id=0, has_side_effects=True, vmem_limit_bytes=56 * 2**20
        ),
        name="coefficients",
    )(rs, inv, vm, ym, mid_cap, vt, yt, top_cap)


def finish_kernel(field, yt, coef, out, last, sem):
    rows, rhs = out.shape
    cols = coef.shape[0]
    done = rhs - cols
    tile = rows // 4
    left = pltpu.make_async_copy(
        field.at[:, pl.ds(0, done)], out.at[:, pl.ds(0, done)], sem.at[4]
    )
    left.start()
    factor = right3(coef[...], 1)
    copies = []
    for i in range(4):
        at = slice(i * tile, (i + 1) * tile)
        last[at, :] = field[at, done:] - dot(left3(yt[at, :]), factor, NT)
        copy = pltpu.make_async_copy(
            last.at[pl.ds(i * tile, tile)],
            out.at[pl.ds(i * tile, tile), pl.ds(done, cols)],
            sem.at[i],
        )
        copy.start()
        copies.append(copy)
    left.wait()
    for copy in copies:
        copy.wait()


def finish(field, yt, coef):
    rows, rhs = field.shape
    return pl.pallas_call(
        finish_kernel,
        out_shape=jax.ShapeDtypeStruct((rows, rhs), jnp.float32),
        in_specs=[pl.BlockSpec(memory_space=pltpu.VMEM)] * 3,
        out_specs=pl.BlockSpec(memory_space=pltpu.HBM),
        scratch_shapes=[
            pltpu.VMEM((rows, coef.shape[0]), jnp.float32),
            pltpu.SemaphoreType.DMA((5,)),
        ],
        compiler_params=pltpu.CompilerParams(vmem_limit_bytes=16 * 2**20),
        name="finish",
    )(field, yt, coef)


def per_device(
    n, right_sides, leaf_inverse, mid_proj, mid_basis, mid_cap, top_proj, top_basis, top_cap
):
    field, basis, coef = coefficients(
        n, right_sides, leaf_inverse, mid_proj, mid_basis, mid_cap, top_proj, top_basis, top_cap
    )
    return finish(field, basis, coef)


def solution(mesh):
    placed = (
        P("rows", None),
        P("rows", None),
        P("rows", None),
        P("rows", None),
        P(),
        P("rows", None),
        P("rows", None),
        P(),
    )
    return jax.shard_map(
        functools.partial(per_device, mesh.shape["rows"]),
        mesh=mesh,
        in_specs=placed,
        out_specs=P("rows", None),
        check_vma=False,
    )
```

```python
import functools

import jax
import jax.numpy as jnp
from jax import lax
from jax.experimental import pallas as pl
from jax.experimental.pallas import tpu as pltpu
from jax.sharding import PartitionSpec as P

MESH = pl.DeviceIdType.MESH
GROUPS = 2
NN = (((1,), (0,)), ((), ()))
NT = (((1,), (1,)), ((), ()))


def split(value):
    high = value.astype(jnp.bfloat16)
    return high, (value - high.astype(jnp.float32)).astype(jnp.bfloat16)


def both_parts(value):
    high, low = split(value)
    return jnp.stack([high, low])


def small_dot(value, parts, dims):
    count = value.shape[0]
    high = value.astype(jnp.bfloat16).astype(jnp.float32)
    stacked = jnp.concatenate([high, value - high], axis=0).astype(jnp.bfloat16)
    wide = dot(stacked, parts[0], dims)
    return wide[:count] + (wide[count:] + dot(high.astype(jnp.bfloat16), parts[1], dims))


def left3(value, axis=1):
    high, low = split(value)
    return jnp.concatenate([high, high, low], axis=axis)


def right3(value, axis):
    high, low = split(value)
    return jnp.concatenate([high, low, high], axis=axis)


def dot(left, right, dims):
    return lax.dot_general(left, right, dims, preferred_element_type=jnp.float32)


def flip(number, mask):
    bit = 1
    while bit <= mask:
        if mask & bit:
            number = number + (1 - 2 * (number // bit % 2)) * bit
        bit *= 2
    return number


def coef_kernel(
    n, leaf, rank,
    rs_hbm, inv_hbm, vm_hbm, ym_hbm, mid_cap, vt_hbm, yt_hbm, top_cap,
    field, basis, coef_last,
    rs, inv, vm, vt, cap, tcap,
    inv3, v3, cap2, tcap2, d2, factor3,
    proj, part, part_in, chip_sum, chip_in, pair, top_p, coef,
    d_part, d_part_in, d_sum, d_in, d_full,
    load_sem, cap_sem, send_sem, recv_sem,
):
    m = n // 4
    chips = m // 2
    me = lax.axis_index("rows")
    quarter, place = me // m, me % m
    core, chip = place % 2, place // 2
    half, side = quarter // 2, quarter % 2
    partner = me + 1 - 2 * core
    sibling = me + m * (1 - 2 * side)
    across = me + 2 * m * (1 - 2 * half)
    rows, rhs = rs.shape
    blocks = rows // leaf
    cols = rhs // GROUPS
    hr = cols // 2
    w = cols // m
    wd = rank // m
    hd = rank // 2

    def on_chip(d):
        return me + 2 * (flip(chip, d) - chip)

    def ds(start, size):
        return pl.ds(pl.multiple_of(start, 8), size)

    def columns(g):
        return pl.ds(pl.multiple_of(g * cols, cols), cols)

    loads = (
        (ym_hbm, basis.at[0]), (vt_hbm, vt), (inv_hbm, inv), (vm_hbm, vm), (yt_hbm, basis.at[1])
    )

    def load(k, b):
        src, dst = loads[k]
        at = ds(b * leaf, leaf)
        return pltpu.make_async_copy(src.at[at], dst.at[at], load_sem.at[k, b])

    def load_rs(g, b):
        at = (ds(b * leaf, leaf), columns(g))
        return pltpu.make_async_copy(rs_hbm.at[at], rs.at[at], load_sem.at[5 + g, b])

    def load_caps():
        return [
            pltpu.make_async_copy(mid_cap.at[half], cap, cap_sem.at[0]),
            pltpu.make_async_copy(top_cap.at[0, ds(half * rank, rank)], tcap, cap_sem.at[1]),
        ]

    def start(copies):
        for copy in copies:
            copy.start()

    def wait(copies):
        for copy in copies:
            copy.wait()

    start([load(k, b) for b in range(blocks) for k in (0, 1)])
    for b in range(blocks):
        start([load(2, b), load_rs(0, b), load(3, b)])
    start([load_rs(1, b) for b in range(blocks)])
    start(load_caps())
    start([load(4, b) for b in range(blocks)])

    barrier = pltpu.get_barrier_semaphore()
    peers = [partner, sibling, across] + [on_chip(d) for d in range(1, chips)]
    for peer in peers:
        pl.semaphore_signal(barrier, inc=1, device_id=(peer,), device_id_type=MESH)

    sizes = dict(
        a=GROUPS, b=GROUPS * chips, c=GROUPS, x=GROUPS, g=GROUPS * 2 * chips, f=GROUPS * 2,
        da=1, db=chips, dz=1, dg=chips, df=1,
    )
    bases = {}
    for kind, size in sizes.items():
        bases[kind] = sum(sizes[k] for k in bases)

    def remote(kind, sub, src, dst, device):
        at = bases[kind] + sub
        return pltpu.make_async_remote_copy(
            src_ref=src, dst_ref=dst, send_sem=send_sem.at[at], recv_sem=recv_sem.at[at],
            device_id=(device,), device_id_type=MESH,
        )

    others = tuple(reversed(range(1, chips)))

    def spread(kind, sub, view):
        return [remote(kind, sub * chips + d, view, view, on_chip(d)) for d in others]

    def same(kind, sub, view, device):
        return [remote(kind, sub, view, view, device)]

    def d_own():
        return ds((core * chips + chip) * wd, wd)

    def d_core():
        return [remote("da", 0, d_part.at[ds((1 - core) * hd, hd)], d_part_in, partner)]

    def d_chips():
        return [
            remote("db", d, d_sum.at[ds(flip(chip, d) * wd, wd)], d_in.at[d], on_chip(d))
            for d in others
        ]

    def d_sibling():
        return same("dz", 0, d_full.at[side, d_own()], sibling)

    def d_gather():
        return spread("dg", 0, d_full.at[:, d_own()])

    def d_forward():
        return same("df", 0, d_full.at[:, ds(core * hd, hd)], partner)

    def d_one():
        wait(d_core())
        d_sum[...] = d_part[ds(core * hd, hd), :] + d_part_in[...]
        start(d_chips())

    def d_two():
        wait(d_chips())
        total = d_sum[ds(chip * wd, wd), :]
        for d in others:
            total += d_in[d]
        d_full[side, d_own(), :] = total
        start(d_sibling())

    def d_three():
        wait(d_sibling())
        start(d_gather())

    def d_four():
        wait(d_gather())
        start(d_forward())

    def d_five():
        wait(d_forward())
        d2[...] = both_parts(jnp.concatenate([d_full[0], d_full[1]], axis=1))

    def to_core(g):
        return [remote("a", g, part.at[g, ds((1 - core) * hr, hr)], part_in.at[g], partner)]

    def to_chips(g):
        return [
            remote(
                "b", g * chips + d,
                chip_sum.at[g, ds(flip(chip, d) * w, w)], chip_in.at[g, d], on_chip(d),
            )
            for d in others
        ]

    def to_sibling(g):
        return same("c", g, pair.at[g, side], sibling)

    def to_across(g):
        return same("x", g, top_p.at[g, half], across)

    def own(g):
        return ds(g * cols + (core * chips + chip) * w, w)

    def gather(g, level):
        return spread("g", g * 2 + level, coef.at[level, own(g)])

    def forward(g, level):
        return same("f", g * 2 + level, coef.at[level, ds(g * cols + core * hr, hr)], partner)

    def add_core(g):
        wait(to_core(g))
        chip_sum[g] = part[g, ds(core * hr, hr), :] + part_in[g]
        start(to_chips(g))

    def add_chips(g):
        wait(to_chips(g))
        total = chip_sum[g, ds(chip * w, w), :]
        for d in others:
            total += chip_in[g, d]
        pair[g, side] = total
        start(to_sibling(g))

    def middle(g):
        wait(to_sibling(g))
        stacked = jnp.concatenate([pair[g, 1, :, :rank], pair[g, 0, :, :rank]], axis=1)
        both = small_dot(stacked, cap2, NT)
        coef[0, own(g), :] = jnp.where(side == 0, both[:, :rank], both[:, rank:])
        return both

    def cross(g, both):
        total = pair[g, 0, :, rank:] + pair[g, 1, :, rank:]
        top_p[g, half] = total - small_dot(both, d2, NT)
        start(to_across(g))

    def top(g):
        wait(to_across(g))
        stacked = jnp.concatenate([top_p[g, 1], top_p[g, 0]], axis=1)
        coef[1, own(g), :] = small_dot(stacked, tcap2, NT)
        start(gather(g, 1))

    def pass_on(g, level):
        wait(gather(g, level))
        start(forward(g, level))

    def correct_task(task):
        g, level = task // 2, task % 2
        wait(forward(g, level))
        here = columns(g)
        factor3[...] = right3(coef[level, here_rows(g), :], 1)

        def step(b, _):
            at = ds(b * leaf, leaf)
            field[at, here] -= dot(left3(basis[level, at, :]), factor3[...], NT)
            return 0

        lax.fori_loop(0, blocks, step, 0)

    def here_rows(g):
        return ds(g * cols, cols)

    def split_caps():
        wait(load_caps())
        cap2[...] = both_parts(cap[...])
        tcap2[...] = both_parts(tcap[...])

    d_part[...] = jnp.zeros_like(d_part)

    def d_step(b, _):
        at = ds(b * leaf, leaf)
        wait([load(0, b), load(1, b)])
        v = left3(vt[at, :].T)
        v3[b, rank:, :] = v
        d_part[...] += dot(v, right3(basis[0, at, :], 0), NN)
        return 0

    lax.fori_loop(0, blocks, d_step, 0)
    pl.semaphore_wait(barrier, len(peers))
    start(d_core())

    hooks = (
        (1, d_one),
        (blocks - 1, d_two),
        (blocks, d_three),
        (blocks + 1, lambda: add_core(0)),
        (blocks + 2, d_four),
        (blocks + 2, split_caps),
    )

    def leaf_step(i, _):
        for when, hook in hooks:
            pl.when(i == when)(hook)
        g, b = i // blocks, i % blocks
        at = ds(b * leaf, leaf)
        wait([load_rs(g, b)])

        @pl.when(g == 0)
        def _():
            wait([load(2, b), load(3, b)])
            inv3[at, :] = left3(inv[at, :])
            v3[b, :rank, :] = left3(vm[at, :].T)

        @pl.when(b == 0)
        def _():
            proj[...] = jnp.zeros_like(proj)

        out = dot(inv3[at, :], right3(rs[at, columns(g)], 0), NN)
        field[at, columns(g)] = out
        proj[...] += dot(v3[b], right3(out, 0), NN)

        @pl.when(b == blocks - 1)
        def _():
            part[g] = proj[...].T
            start(to_core(g))

        return 0

    lax.fori_loop(0, GROUPS * blocks, leaf_step, 0)
    add_chips(0)
    add_core(1)
    d_five()
    wait([load(4, b) for b in range(blocks)])

    def level_step(g, _):
        both = middle(g)
        start(gather(g, 0))
        cross(g, both)
        pl.when(g == 0)(lambda: add_chips(1))

        @pl.when(g == 1)
        def _():
            pass_on(0, 0)
            correct_task(0)

        top(g)
        return 0

    lax.fori_loop(0, GROUPS, level_step, 0)
    pass_on(0, 1)
    pass_on(1, 0)

    def last_step(task, _):
        pl.when(task == 2)(lambda: pass_on(1, 1))
        correct_task(task)
        return 0

    lax.fori_loop(1, 3, last_step, 0)
    wait(forward(1, 1))
    coef_last[...] = coef[1, cols:, :]


def coefficients(n, rs, inv, vm, ym, mid_cap, vt, yt, top_cap):
    rows, rhs = rs.shape
    leaf = inv.shape[1]
    rank = vm.shape[1]
    m = n // 4
    chips = m // 2
    cols = rhs // GROUPS
    w, wd = cols // m, rank // m
    blocks = rows // leaf
    f32, bf16 = jnp.float32, jnp.bfloat16
    copies = 2 * chips + 3 + GROUPS * (3 * chips + 5)

    def vmem(*shape, dtype=f32):
        return pltpu.VMEM(shape, dtype)

    return pl.pallas_call(
        functools.partial(coef_kernel, n, leaf, rank),
        out_shape=(vmem(rows, rhs), vmem(2, rows, rank), vmem(cols, rank)),
        in_specs=[pl.BlockSpec(memory_space=pltpu.HBM)] * 8,
        out_specs=[pl.BlockSpec(memory_space=pltpu.VMEM)] * 3,
        scratch_shapes=[
            vmem(rows, rhs), vmem(rows, leaf), vmem(rows, rank), vmem(rows, rank),
            vmem(2 * rank, 2 * rank), vmem(rank, 2 * rank),
            vmem(rows, 3 * leaf, dtype=bf16), vmem(blocks, 2 * rank, 3 * leaf, dtype=bf16),
            vmem(2, 2 * rank, 2 * rank, dtype=bf16), vmem(2, rank, 2 * rank, dtype=bf16),
            vmem(2, rank, 2 * rank, dtype=bf16), vmem(cols, 3 * rank, dtype=bf16), vmem(2 * rank, cols),
            vmem(GROUPS, cols, 2 * rank), vmem(GROUPS, cols // 2, 2 * rank),
            vmem(GROUPS, cols // 2, 2 * rank), vmem(GROUPS, chips, w, 2 * rank),
            vmem(GROUPS, 2, w, 2 * rank), vmem(GROUPS, 2, w, rank), vmem(2, rhs, rank),
            vmem(rank, rank), vmem(rank // 2, rank), vmem(rank // 2, rank),
            vmem(chips, wd, rank), vmem(2, rank, rank),
            pltpu.SemaphoreType.DMA((5 + GROUPS, blocks)),
            pltpu.SemaphoreType.DMA((2,)),
            pltpu.SemaphoreType.DMA((copies,)),
            pltpu.SemaphoreType.DMA((copies,)),
        ],
        compiler_params=pltpu.CompilerParams(
            collective_id=0, has_side_effects=True, vmem_limit_bytes=54 * 2**20
        ),
        name="coefficients",
    )(rs, inv, vm, ym, mid_cap, vt, yt, top_cap)


def finish_kernel(field, basis, coef, out, last, factor3, sem):
    rows, rhs = out.shape
    cols = coef.shape[0]
    done = rhs - cols
    tiles = sem.shape[0] - 1
    tile = rows // tiles
    left = pltpu.make_async_copy(
        field.at[:, pl.ds(0, done)], out.at[:, pl.ds(0, done)], sem.at[tiles]
    )
    left.start()
    factor3[...] = right3(coef[...], 1)

    def right(i):
        at = pl.ds(pl.multiple_of(i * tile, tile), tile)
        return at, pltpu.make_async_copy(last.at[at], out.at[at, pl.ds(done, cols)], sem.at[i])

    def step(i, _):
        at, copy = right(i)
        last[at, :] = field[at, done:] - dot(left3(basis[1, at, :]), factor3[...], NT)
        copy.start()
        return 0

    lax.fori_loop(0, tiles, step, 0)
    left.wait()
    for i in range(tiles):
        right(i)[1].wait()


def finish(field, yt, coef):
    rows, rhs = field.shape
    return pl.pallas_call(
        finish_kernel,
        out_shape=jax.ShapeDtypeStruct((rows, rhs), jnp.float32),
        in_specs=[pl.BlockSpec(memory_space=pltpu.VMEM)] * 3,
        out_specs=pl.BlockSpec(memory_space=pltpu.HBM),
        scratch_shapes=[
            pltpu.VMEM((rows, coef.shape[0]), jnp.float32),
            pltpu.VMEM((coef.shape[0], 3 * coef.shape[1]), jnp.bfloat16),
            pltpu.SemaphoreType.DMA((5,)),
        ],
        compiler_params=pltpu.CompilerParams(vmem_limit_bytes=16 * 2**20),
        name="finish",
    )(field, yt, coef)


def per_device(
    n, right_sides, leaf_inverse, mid_proj, mid_basis, mid_cap, top_proj, top_basis, top_cap
):
    field, basis, coef = coefficients(
        n, right_sides, leaf_inverse, mid_proj, mid_basis, mid_cap, top_proj, top_basis, top_cap
    )
    return finish(field, basis, coef)


def solution(mesh):
    placed = (
        P("rows", None),
        P("rows", None),
        P("rows", None),
        P("rows", None),
        P(),
        P("rows", None),
        P("rows", None),
        P(),
    )
    return jax.shard_map(
        functools.partial(per_device, mesh.shape["rows"]),
        mesh=mesh,
        in_specs=placed,
        out_specs=P("rows", None),
        check_vma=False,
    )
```

```python
import functools

import jax
import jax.numpy as jnp
from jax import lax
from jax.experimental import pallas as pl
from jax.experimental.pallas import tpu as pltpu
from jax.sharding import PartitionSpec as P

MESH = pl.DeviceIdType.MESH
GROUPS = 2
NN = (((1,), (0,)), ((), ()))
NT = (((1,), (1,)), ((), ()))


def split(value):
    high = value.astype(jnp.bfloat16)
    return high, (value - high.astype(jnp.float32)).astype(jnp.bfloat16)


def both_parts(value):
    high, low = split(value)
    return jnp.stack([high, low])


def small_dot(value, parts, dims):
    count = value.shape[0]
    high = value.astype(jnp.bfloat16).astype(jnp.float32)
    stacked = jnp.concatenate([high, value - high], axis=0).astype(jnp.bfloat16)
    wide = dot(stacked, parts[0], dims)
    return wide[:count] + (wide[count:] + dot(high.astype(jnp.bfloat16), parts[1], dims))


def left3(value, axis=1):
    high, low = split(value)
    return jnp.concatenate([high, high, low], axis=axis)


def right3(value, axis):
    high, low = split(value)
    return jnp.concatenate([high, low, high], axis=axis)


def dot(left, right, dims):
    return lax.dot_general(left, right, dims, preferred_element_type=jnp.float32)


def flip(number, mask):
    bit = 1
    while bit <= mask:
        if mask & bit:
            number = number + (1 - 2 * (number // bit % 2)) * bit
        bit *= 2
    return number


def coef_kernel(
    n, leaf, rank,
    rs_hbm, inv_hbm, vm_hbm, ym_hbm, mid_cap, vt_hbm, yt_hbm, top_cap,
    field, yt, coef_top,
    rs, inv, vm, vt, ym, cap, tcap,
    field3, v3, cap2, tcap2, d2, factor3,
    part, part_in, chip_sum, chip_in, pair, top_p, coef,
    d_part, d_part_in, d_sum, d_in, d_full,
    load_sem, cap_sem, send_sem, recv_sem,
):
    m = n // 4
    chips = m // 2
    me = lax.axis_index("rows")
    quarter, place = me // m, me % m
    core, chip = place % 2, place // 2
    half, side = quarter // 2, quarter % 2
    partner = me + 1 - 2 * core
    sibling = me + m * (1 - 2 * side)
    across = me + 2 * m * (1 - 2 * half)
    rows, rhs = rs.shape
    blocks = rows // leaf
    cols = rhs // GROUPS
    hr = cols // 2
    w = cols // m
    wd = rank // m
    hd = rank // 2

    def on_chip(d):
        return me + 2 * (flip(chip, d) - chip)

    def ds(start, size):
        return pl.ds(pl.multiple_of(start, 8), size)

    loads = (
        (ym_hbm, ym), (vt_hbm, vt), (inv_hbm, inv), (rs_hbm, rs), (vm_hbm, vm), (yt_hbm, yt)
    )

    def load(k, b):
        src, dst = loads[k]
        at = ds(b * leaf, leaf)
        return pltpu.make_async_copy(src.at[at], dst.at[at], load_sem.at[k, b])

    def load_caps():
        return [
            pltpu.make_async_copy(mid_cap.at[half], cap, cap_sem.at[0]),
            pltpu.make_async_copy(top_cap.at[0, ds(half * rank, rank)], tcap, cap_sem.at[1]),
        ]

    def start(copies):
        for copy in copies:
            copy.start()

    def wait(copies):
        for copy in copies:
            copy.wait()

    start([load(k, b) for b in range(blocks) for k in (0, 1)])
    start([load(k, b) for b in range(blocks) for k in (2, 3, 4)])
    start(load_caps())
    start([load(5, b) for b in range(blocks)])

    barrier = pltpu.get_barrier_semaphore()
    peers = [partner, sibling, across] + [on_chip(d) for d in range(1, chips)]
    for peer in peers:
        pl.semaphore_signal(barrier, inc=1, device_id=(peer,), device_id_type=MESH)

    sizes = dict(
        a=GROUPS, b=GROUPS * chips, c=GROUPS, x=GROUPS, g=GROUPS * 2 * chips, f=GROUPS * 2,
        da=1, db=chips, dz=1, dg=chips, df=1,
    )
    bases = {}
    for kind, size in sizes.items():
        bases[kind] = sum(sizes[k] for k in bases)

    def remote(kind, sub, src, dst, device):
        at = bases[kind] + sub
        return pltpu.make_async_remote_copy(
            src_ref=src, dst_ref=dst, send_sem=send_sem.at[at], recv_sem=recv_sem.at[at],
            device_id=(device,), device_id_type=MESH,
        )

    others = tuple(reversed(range(1, chips)))

    def spread(kind, sub, view):
        return [remote(kind, sub * chips + d, view, view, on_chip(d)) for d in others]

    def same(kind, sub, view, device):
        return [remote(kind, sub, view, view, device)]

    def d_own():
        return ds((core * chips + chip) * wd, wd)

    def d_core():
        return [remote("da", 0, d_part.at[ds((1 - core) * hd, hd)], d_part_in, partner)]

    def d_chips():
        return [
            remote("db", d, d_sum.at[ds(flip(chip, d) * wd, wd)], d_in.at[d], on_chip(d))
            for d in others
        ]

    def d_sibling():
        return same("dz", 0, d_full.at[side, d_own()], sibling)

    def d_gather():
        return spread("dg", 0, d_full.at[:, d_own()])

    def d_forward():
        return same("df", 0, d_full.at[:, ds(core * hd, hd)], partner)

    def d_one():
        wait(d_core())
        d_sum[...] = d_part[ds(core * hd, hd), :] + d_part_in[...]
        start(d_chips())

    def d_two():
        wait(d_chips())
        total = d_sum[ds(chip * wd, wd), :]
        for d in others:
            total += d_in[d]
        d_full[side, d_own(), :] = total
        start(d_sibling())

    def d_three():
        wait(d_sibling())
        start(d_gather())

    def d_four():
        wait(d_gather())
        start(d_forward())

    def d_five():
        wait(d_forward())
        d2[...] = both_parts(jnp.concatenate([d_full[0], d_full[1]], axis=0))

    def to_core(g):
        return [remote("a", g, part.at[g, ds((1 - core) * hr, hr)], part_in.at[g], partner)]

    def to_chips(g):
        return [
            remote(
                "b", g * chips + d,
                chip_sum.at[g, ds(flip(chip, d) * w, w)], chip_in.at[g, d], on_chip(d),
            )
            for d in others
        ]

    def to_sibling(g):
        return same("c", g, pair.at[g, side], sibling)

    def to_across(g):
        return same("x", g, top_p.at[g, half], across)

    def own(g):
        return ds(g * cols + (core * chips + chip) * w, w)

    def gather(g, level):
        return spread("g", g * 2 + level, coef.at[level, own(g)])

    def forward(g, level):
        return same("f", g * 2 + level, coef.at[level, ds(g * cols + core * hr, hr)], partner)

    def add_core(g):
        wait(to_core(g))
        chip_sum[g] = part[g, ds(core * hr, hr), :] + part_in[g]
        start(to_chips(g))

    def add_chips(g):
        wait(to_chips(g))
        total = chip_sum[g, ds(chip * w, w), :]
        for d in others:
            total += chip_in[g, d]
        pair[g, side] = total
        start(to_sibling(g))

    def middle(g):
        wait(to_sibling(g))
        stacked = jnp.concatenate([pair[g, 1, :, :rank], pair[g, 0, :, :rank]], axis=1)
        both = small_dot(stacked, cap2, NT)
        coef[0, own(g), :] = jnp.where(side == 0, both[:, :rank], both[:, rank:])
        return both

    def cross(g, both):
        total = pair[g, 0, :, rank:] + pair[g, 1, :, rank:]
        top_p[g, half] = total - small_dot(both, d2, NN)
        start(to_across(g))

    def top(g):
        wait(to_across(g))
        stacked = jnp.concatenate([top_p[g, 1], top_p[g, 0]], axis=1)
        coef[1, own(g), :] = small_dot(stacked, tcap2, NT)
        start(gather(g, 1))

    def pass_on(g, level):
        wait(gather(g, level))
        start(forward(g, level))

    def correct_mid():
        factor3[...] = right3(coef[0], 1)

        def step(i, _):
            for b in (2 * i, 2 * i + 1):
                at = ds(b * leaf, leaf)
                field[at, :] -= dot(left3(ym[at, :]), factor3[...], NT)
            return 0

        lax.fori_loop(0, blocks // 2, step, 0)

    def project(g, hooks):
        part[g] = jnp.zeros_like(part[g])

        def step(i, _):
            for when, hook in hooks:
                pl.when(i == when)(hook)
            b, here = 2 * i, slice(g * cols, (g + 1) * cols)
            part[g] += dot(field3[b, here, :], v3[b], NN) + dot(
                field3[b + 1, here, :], v3[b + 1], NN
            )
            return 0

        lax.fori_loop(0, blocks // 2, step, 0)
        start(to_core(g))

    def split_caps():
        wait(load_caps())
        cap2[...] = both_parts(cap[...])
        tcap2[...] = both_parts(tcap[...])

    d_part[...] = jnp.zeros_like(d_part)

    def d_step(b, _):
        at = ds(b * leaf, leaf)
        wait([load(0, b), load(1, b)])
        v = right3(vt[at, :], 0)
        v3[b, :, rank:] = v
        d_part[...] += dot(left3(ym[at, :].T), v, NN)
        return 0

    lax.fori_loop(0, blocks, d_step, 0)
    pl.semaphore_wait(barrier, len(peers))
    start(d_core())

    def leaf_step(i, _):
        pl.when(i == 1)(d_one)
        for b in (2 * i, 2 * i + 1):
            at = ds(b * leaf, leaf)
            wait([load(2, b), load(3, b), load(4, b)])
            out = dot(left3(inv[at, :]), right3(rs[at, :], 0), NN)
            field[at, :] = out
            field3[b] = left3(out.T)
            v3[b, :, :rank] = right3(vm[at, :], 0)
        return 0

    lax.fori_loop(0, blocks // 2, leaf_step, 0)
    d_two()
    project(0, ())
    d_three()
    project(1, ((1, lambda: add_core(0)),))
    split_caps()
    add_core(1)
    d_four()
    add_chips(0)
    d_five()

    def level_step(g, _):
        both = middle(g)
        start(gather(g, 0))
        cross(g, both)

        @pl.when(g == 0)
        def _():
            add_chips(1)

        @pl.when(g == 1)
        def _():
            pass_on(0, 0)

        top(g)
        return 0

    lax.fori_loop(0, GROUPS, level_step, 0)
    pass_on(1, 0)
    pass_on(0, 1)
    wait(forward(0, 0) + forward(1, 0))
    wait([load(5, b) for b in range(blocks)])
    correct_mid()
    pass_on(1, 1)
    wait(forward(0, 1) + forward(1, 1))
    coef_top[...] = coef[1]


def coefficients(n, rs, inv, vm, ym, mid_cap, vt, yt, top_cap):
    rows, rhs = rs.shape
    leaf = inv.shape[1]
    rank = vm.shape[1]
    m = n // 4
    chips = m // 2
    cols = rhs // GROUPS
    w, wd = cols // m, rank // m
    blocks = rows // leaf
    f32, bf16 = jnp.float32, jnp.bfloat16
    copies = 2 * chips + 3 + GROUPS * (3 * chips + 5)

    def vmem(*shape, dtype=f32):
        return pltpu.VMEM(shape, dtype)

    return pl.pallas_call(
        functools.partial(coef_kernel, n, leaf, rank),
        out_shape=(vmem(rows, rhs), vmem(rows, rank), vmem(rhs, rank)),
        in_specs=[pl.BlockSpec(memory_space=pltpu.HBM)] * 8,
        out_specs=[pl.BlockSpec(memory_space=pltpu.VMEM)] * 3,
        scratch_shapes=[
            vmem(rows, rhs), vmem(rows, leaf), vmem(rows, rank), vmem(rows, rank),
            vmem(rows, rank), vmem(2 * rank, 2 * rank), vmem(rank, 2 * rank),
            vmem(blocks, rhs, 3 * leaf, dtype=bf16), vmem(blocks, 3 * leaf, 2 * rank, dtype=bf16),
            vmem(2, 2 * rank, 2 * rank, dtype=bf16), vmem(2, rank, 2 * rank, dtype=bf16),
            vmem(2, 2 * rank, rank, dtype=bf16), vmem(rhs, 3 * rank, dtype=bf16),
            vmem(GROUPS, cols, 2 * rank), vmem(GROUPS, cols // 2, 2 * rank),
            vmem(GROUPS, cols // 2, 2 * rank), vmem(GROUPS, chips, w, 2 * rank),
            vmem(GROUPS, 2, w, 2 * rank), vmem(GROUPS, 2, w, rank), vmem(2, rhs, rank),
            vmem(rank, rank), vmem(rank // 2, rank), vmem(rank // 2, rank),
            vmem(chips, wd, rank), vmem(2, rank, rank),
            pltpu.SemaphoreType.DMA((6, blocks)),
            pltpu.SemaphoreType.DMA((2,)),
            pltpu.SemaphoreType.DMA((copies,)),
            pltpu.SemaphoreType.DMA((copies,)),
        ],
        compiler_params=pltpu.CompilerParams(
            collective_id=0, has_side_effects=True, vmem_limit_bytes=55 * 2**20
        ),
        name="coefficients",
    )(rs, inv, vm, ym, mid_cap, vt, yt, top_cap)


def finish_kernel(field, yt, coef, out, last, sem):
    tiles = sem.shape[0]
    tile = out.shape[0] // tiles
    factor = right3(coef[...], 1)
    copies = []
    for i in range(tiles):
        at = pl.ds(i * tile, tile)
        last[at, :] = field[at, :] - dot(left3(yt[at, :]), factor, NT)
        copies.append(pltpu.make_async_copy(last.at[at], out.at[at], sem.at[i]))
        copies[-1].start()
    for copy in copies:
        copy.wait()


def finish(field, yt, coef):
    rows, rhs = field.shape
    return pl.pallas_call(
        finish_kernel,
        out_shape=jax.ShapeDtypeStruct((rows, rhs), jnp.float32),
        in_specs=[pl.BlockSpec(memory_space=pltpu.VMEM)] * 3,
        out_specs=pl.BlockSpec(memory_space=pltpu.HBM),
        scratch_shapes=[
            pltpu.VMEM((rows, rhs), jnp.float32),
            pltpu.SemaphoreType.DMA((4,)),
        ],
        compiler_params=pltpu.CompilerParams(vmem_limit_bytes=24 * 2**20),
        name="finish",
    )(field, yt, coef)


def per_device(
    n, right_sides, leaf_inverse, mid_proj, mid_basis, mid_cap, top_proj, top_basis, top_cap
):
    field, basis, coef = coefficients(
        n, right_sides, leaf_inverse, mid_proj, mid_basis, mid_cap, top_proj, top_basis, top_cap
    )
    return finish(field, basis, coef)


def solution(mesh):
    placed = (
        P("rows", None),
        P("rows", None),
        P("rows", None),
        P("rows", None),
        P(),
        P("rows", None),
        P("rows", None),
        P(),
    )
    return jax.shard_map(
        functools.partial(per_device, mesh.shape["rows"]),
        mesh=mesh,
        in_specs=placed,
        out_specs=P("rows", None),
        check_vma=False,
    )
```

```python
import functools

import jax
import jax.numpy as jnp
from jax import lax
from jax.experimental import pallas as pl
from jax.experimental.pallas import tpu as pltpu
from jax.sharding import PartitionSpec as P

MESH = pl.DeviceIdType.MESH
GROUPS = 2
NN = (((1,), (0,)), ((), ()))
NT = (((1,), (1,)), ((), ()))


def split(value):
    high = value.astype(jnp.bfloat16)
    return high, (value - high.astype(jnp.float32)).astype(jnp.bfloat16)


def both_parts(value):
    high, low = split(value)
    return jnp.stack([high, low])


def small_dot(value, parts, dims):
    count = value.shape[0]
    high = value.astype(jnp.bfloat16).astype(jnp.float32)
    stacked = jnp.concatenate([high, value - high], axis=0).astype(jnp.bfloat16)
    wide = dot(stacked, parts[0], dims)
    return wide[:count] + (wide[count:] + dot(high.astype(jnp.bfloat16), parts[1], dims))


def left3(value, axis=1):
    high, low = split(value)
    return jnp.concatenate([high, high, low], axis=axis)


def right3(value, axis):
    high, low = split(value)
    return jnp.concatenate([high, low, high], axis=axis)


def dot(left, right, dims):
    return lax.dot_general(left, right, dims, preferred_element_type=jnp.float32)


def flip(number, mask):
    bit = 1
    while bit <= mask:
        if mask & bit:
            number = number + (1 - 2 * (number // bit % 2)) * bit
        bit *= 2
    return number


def coef_kernel(
    n, leaf, rank,
    rs_hbm, inv_hbm, vm_hbm, ym_hbm, mid_cap, vt_hbm, yt_hbm, top_cap,
    field, yt, coef_top,
    rs, inv, vm, vt, ym, cap, tcap,
    field3, v3, cap2, tcap2, d2, factor3,
    part, part_in, chip_sum, chip_in, pair, top_p, coef,
    d_part, d_part_in, d_sum, d_in, d_full,
    load_sem, cap_sem, send_sem, recv_sem,
):
    m = n // 4
    chips = m // 2
    me = lax.axis_index("rows")
    quarter, place = me // m, me % m
    core, chip = place % 2, place // 2
    half, side = quarter // 2, quarter % 2
    partner = me + 1 - 2 * core
    sibling = me + m * (1 - 2 * side)
    across = me + 2 * m * (1 - 2 * half)
    rows, rhs = rs.shape
    blocks = rows // leaf
    cols = rhs // GROUPS
    hr = cols // 2
    w = cols // m
    wd = rank // m
    hd = rank // 2

    def on_chip(d):
        return me + 2 * (flip(chip, d) - chip)

    def ds(start, size):
        return pl.ds(pl.multiple_of(start, 8), size)

    loads = (
        (ym_hbm, ym), (vt_hbm, vt), (inv_hbm, inv), (rs_hbm, rs), (vm_hbm, vm), (yt_hbm, yt)
    )

    def load(k, b):
        src, dst = loads[k]
        at = ds(b * leaf, leaf)
        return pltpu.make_async_copy(src.at[at], dst.at[at], load_sem.at[k, b])

    def load_caps():
        return [
            pltpu.make_async_copy(mid_cap.at[half], cap, cap_sem.at[0]),
            pltpu.make_async_copy(top_cap.at[0, ds(half * rank, rank)], tcap, cap_sem.at[1]),
        ]

    def start(copies):
        for copy in copies:
            copy.start()

    def wait(copies):
        for copy in copies:
            copy.wait()

    start([load(k, b) for b in range(blocks) for k in (0, 1)])
    start([load(k, b) for b in range(blocks) for k in (2, 3, 4)])
    start(load_caps())
    start([load(5, b) for b in range(blocks)])

    barrier = pltpu.get_barrier_semaphore()
    peers = [partner, sibling, across] + [on_chip(d) for d in range(1, chips)]
    for peer in peers:
        pl.semaphore_signal(barrier, inc=1, device_id=(peer,), device_id_type=MESH)

    sizes = dict(
        a=GROUPS, b=GROUPS * chips, c=GROUPS, x=GROUPS, g=GROUPS * 2 * chips, f=GROUPS * 2,
        da=1, db=chips, dz=1, dg=chips, df=1,
    )
    bases = {}
    for kind, size in sizes.items():
        bases[kind] = sum(sizes[k] for k in bases)

    def remote(kind, sub, src, dst, device):
        at = bases[kind] + sub
        return pltpu.make_async_remote_copy(
            src_ref=src, dst_ref=dst, send_sem=send_sem.at[at], recv_sem=recv_sem.at[at],
            device_id=(device,), device_id_type=MESH,
        )

    others = tuple(reversed(range(1, chips)))

    def spread(kind, sub, view):
        return [remote(kind, sub * chips + d, view, view, on_chip(d)) for d in others]

    def same(kind, sub, view, device):
        return [remote(kind, sub, view, view, device)]

    def d_own():
        return ds((core * chips + chip) * wd, wd)

    def d_core():
        return [remote("da", 0, d_part.at[ds((1 - core) * hd, hd)], d_part_in, partner)]

    def d_chips():
        return [
            remote("db", d, d_sum.at[ds(flip(chip, d) * wd, wd)], d_in.at[d], on_chip(d))
            for d in others
        ]

    def d_sibling():
        return same("dz", 0, d_full.at[side, d_own()], sibling)

    def d_gather():
        return spread("dg", 0, d_full.at[:, d_own()])

    def d_forward():
        return same("df", 0, d_full.at[:, ds(core * hd, hd)], partner)

    def d_one():
        wait(d_core())
        d_sum[...] = d_part[ds(core * hd, hd), :] + d_part_in[...]
        start(d_chips())

    def d_two():
        wait(d_chips())
        total = d_sum[ds(chip * wd, wd), :]
        for d in others:
            total += d_in[d]
        d_full[side, d_own(), :] = total
        start(d_sibling())

    def d_three():
        wait(d_sibling())
        start(d_gather())

    def d_four():
        wait(d_gather())
        start(d_forward())

    def d_five():
        wait(d_forward())
        d2[...] = both_parts(jnp.concatenate([d_full[0], d_full[1]], axis=0))

    def to_core(g):
        return [remote("a", g, part.at[g, ds((1 - core) * hr, hr)], part_in.at[g], partner)]

    def to_chips(g):
        return [
            remote(
                "b", g * chips + d,
                chip_sum.at[g, ds(flip(chip, d) * w, w)], chip_in.at[g, d], on_chip(d),
            )
            for d in others
        ]

    def to_sibling(g):
        return same("c", g, pair.at[g, side], sibling)

    def to_across(g):
        return same("x", g, top_p.at[g, half], across)

    def own(g):
        return ds(g * cols + (core * chips + chip) * w, w)

    def gather(g, level):
        return spread("g", g * 2 + level, coef.at[level, own(g)])

    def forward(g, level):
        return same("f", g * 2 + level, coef.at[level, ds(g * cols + core * hr, hr)], partner)

    def add_core(g):
        wait(to_core(g))
        chip_sum[g] = part[g, ds(core * hr, hr), :] + part_in[g]
        start(to_chips(g))

    def add_chips(g):
        wait(to_chips(g))
        total = chip_sum[g, ds(chip * w, w), :]
        for d in others:
            total += chip_in[g, d]
        pair[g, side] = total
        start(to_sibling(g))

    def middle(g):
        wait(to_sibling(g))
        stacked = jnp.concatenate([pair[g, 1, :, :rank], pair[g, 0, :, :rank]], axis=1)
        both = small_dot(stacked, cap2, NT)
        coef[0, own(g), :] = jnp.where(side == 0, both[:, :rank], both[:, rank:])
        return both

    def cross(g, both):
        total = pair[g, 0, :, rank:] + pair[g, 1, :, rank:]
        top_p[g, half] = total - small_dot(both, d2, NN)
        start(to_across(g))

    def top(g):
        wait(to_across(g))
        stacked = jnp.concatenate([top_p[g, 1], top_p[g, 0]], axis=1)
        coef[1, own(g), :] = small_dot(stacked, tcap2, NT)
        start(gather(g, 1))

    def pass_on(g, level):
        wait(gather(g, level))
        start(forward(g, level))

    def correct_mid():
        factor3[...] = right3(coef[0], 1)

        def step(i, _):
            for b in (2 * i, 2 * i + 1):
                at = ds(b * leaf, leaf)
                field[at, :] -= dot(left3(ym[at, :]), factor3[...], NT)
            return 0

        lax.fori_loop(0, blocks // 2, step, 0)

    def project(g, hooks):
        part[g] = jnp.zeros_like(part[g])

        def step(i, _):
            for when, hook in hooks:
                pl.when(i == when)(hook)
            b, here = 2 * i, slice(g * cols, (g + 1) * cols)
            part[g] += dot(field3[b, here, :], v3[b], NN) + dot(
                field3[b + 1, here, :], v3[b + 1], NN
            )
            return 0

        lax.fori_loop(0, blocks // 2, step, 0)
        start(to_core(g))

    def split_caps():
        wait(load_caps())
        cap2[...] = both_parts(cap[...])
        tcap2[...] = both_parts(tcap[...])

    d_part[...] = jnp.zeros_like(d_part)

    def d_step(b, _):
        at = ds(b * leaf, leaf)
        wait([load(0, b), load(1, b)])
        v = right3(vt[at, :], 0)
        v3[b, :, rank:] = v
        d_part[...] += dot(left3(ym[at, :].T), v, NN)
        return 0

    lax.fori_loop(0, blocks, d_step, 0)
    pl.semaphore_wait(barrier, len(peers))
    start(d_core())

    hooks = {1: d_one, blocks - 1: d_two}
    for b in range(blocks):
        hooks.get(b, lambda: None)()
        at = slice(b * leaf, (b + 1) * leaf)
        wait([load(2, b), load(3, b), load(4, b)])
        out = dot(left3(inv[at, :]), right3(rs[at, :], 0), NN)
        field[at, :] = out
        field3[b] = left3(out.T)
        v3[b, :, :rank] = right3(vm[at, :], 0)
    d_three()
    project(0, ())
    d_four()
    project(1, ((1, lambda: add_core(0)),))
    split_caps()
    add_core(1)
    add_chips(0)
    d_five()
    both = middle(0)
    cross(0, both)
    add_chips(1)
    start(gather(0, 0))
    top(0)
    both = middle(1)
    start(gather(1, 0))
    cross(1, both)
    pass_on(0, 0)
    top(1)
    pass_on(1, 0)
    pass_on(0, 1)
    wait(forward(0, 0) + forward(1, 0))
    wait([load(5, b) for b in range(blocks)])
    correct_mid()
    pass_on(1, 1)
    wait(forward(0, 1) + forward(1, 1))
    coef_top[...] = coef[1]


def coefficients(n, rs, inv, vm, ym, mid_cap, vt, yt, top_cap):
    rows, rhs = rs.shape
    leaf = inv.shape[1]
    rank = vm.shape[1]
    m = n // 4
    chips = m // 2
    cols = rhs // GROUPS
    w, wd = cols // m, rank // m
    blocks = rows // leaf
    f32, bf16 = jnp.float32, jnp.bfloat16
    copies = 2 * chips + 3 + GROUPS * (3 * chips + 5)

    def vmem(*shape, dtype=f32):
        return pltpu.VMEM(shape, dtype)

    return pl.pallas_call(
        functools.partial(coef_kernel, n, leaf, rank),
        out_shape=(vmem(rows, rhs), vmem(rows, rank), vmem(rhs, rank)),
        in_specs=[pl.BlockSpec(memory_space=pltpu.HBM)] * 8,
        out_specs=[pl.BlockSpec(memory_space=pltpu.VMEM)] * 3,
        scratch_shapes=[
            vmem(rows, rhs), vmem(rows, leaf), vmem(rows, rank), vmem(rows, rank),
            vmem(rows, rank), vmem(2 * rank, 2 * rank), vmem(rank, 2 * rank),
            vmem(blocks, rhs, 3 * leaf, dtype=bf16), vmem(blocks, 3 * leaf, 2 * rank, dtype=bf16),
            vmem(2, 2 * rank, 2 * rank, dtype=bf16), vmem(2, rank, 2 * rank, dtype=bf16),
            vmem(2, 2 * rank, rank, dtype=bf16), vmem(rhs, 3 * rank, dtype=bf16),
            vmem(GROUPS, cols, 2 * rank), vmem(GROUPS, cols // 2, 2 * rank),
            vmem(GROUPS, cols // 2, 2 * rank), vmem(GROUPS, chips, w, 2 * rank),
            vmem(GROUPS, 2, w, 2 * rank), vmem(GROUPS, 2, w, rank), vmem(2, rhs, rank),
            vmem(rank, rank), vmem(rank // 2, rank), vmem(rank // 2, rank),
            vmem(chips, wd, rank), vmem(2, rank, rank),
            pltpu.SemaphoreType.DMA((6, blocks)),
            pltpu.SemaphoreType.DMA((2,)),
            pltpu.SemaphoreType.DMA((copies,)),
            pltpu.SemaphoreType.DMA((copies,)),
        ],
        compiler_params=pltpu.CompilerParams(
            collective_id=0, has_side_effects=True, vmem_limit_bytes=55 * 2**20
        ),
        name="coefficients",
    )(rs, inv, vm, ym, mid_cap, vt, yt, top_cap)


def finish_kernel(field, yt, coef, out, last, sem):
    tiles = sem.shape[0]
    tile = out.shape[0] // tiles
    factor = right3(coef[...], 1)
    copies = []
    for i in range(tiles):
        at = pl.ds(i * tile, tile)
        last[at, :] = field[at, :] - dot(left3(yt[at, :]), factor, NT)
        copies.append(pltpu.make_async_copy(last.at[at], out.at[at], sem.at[i]))
        copies[-1].start()
    for copy in copies:
        copy.wait()


def finish(field, yt, coef):
    rows, rhs = field.shape
    return pl.pallas_call(
        finish_kernel,
        out_shape=jax.ShapeDtypeStruct((rows, rhs), jnp.float32),
        in_specs=[pl.BlockSpec(memory_space=pltpu.VMEM)] * 3,
        out_specs=pl.BlockSpec(memory_space=pltpu.HBM),
        scratch_shapes=[
            pltpu.VMEM((rows, rhs), jnp.float32),
            pltpu.SemaphoreType.DMA((4,)),
        ],
        compiler_params=pltpu.CompilerParams(vmem_limit_bytes=24 * 2**20),
        name="finish",
    )(field, yt, coef)


def per_device(
    n, right_sides, leaf_inverse, mid_proj, mid_basis, mid_cap, top_proj, top_basis, top_cap
):
    field, basis, coef = coefficients(
        n, right_sides, leaf_inverse, mid_proj, mid_basis, mid_cap, top_proj, top_basis, top_cap
    )
    return finish(field, basis, coef)


def solution(mesh):
    placed = (
        P("rows", None),
        P("rows", None),
        P("rows", None),
        P("rows", None),
        P(),
        P("rows", None),
        P("rows", None),
        P(),
    )
    return jax.shard_map(
        functools.partial(per_device, mesh.shape["rows"]),
        mesh=mesh,
        in_specs=placed,
        out_specs=P("rows", None),
        check_vma=False,
    )
```
